32 devices in a mesh: dp: 8 (over z, y), fsdp: 4 (over x, core).
Axes of the slice: x: 2, y: 2, z: 4, core: 2. Of those that a mesh axis runs over, the one named last changes fastest.
Arguments:
- tokens: bfloat16 [32768, 768], P(('dp', 'fsdp')), may hold values from -6 to 6
- ends: int32 [32, 24], P(('dp', 'fsdp')), may hold values from 20 to 1023, as said below
- cot_out: bfloat16 [32768, 768], P(('dp', 'fsdp')), may hold values from -6 to 6
- cot_pooled: float32 [32, 24, 768], P(('dp', 'fsdp')), may hold values from -6 to 6
- w_qkv: float32 [768, 2304], P(('dp', 'fsdp')), may hold values from -0.21875 to 0.21875
- w_out: float32 [768, 768], P(('dp', 'fsdp')), may hold values from -1.25 to 1.25
- w_up: float32 [768, 3072], P(('dp', 'fsdp')), may hold values from -0.21875 to 0.21875
- w_down: float32 [3072, 768], P(('dp', 'fsdp')), may hold values from -0.109375 to 0.109375
- vectors: float32 [768, 8], P(('dp', 'fsdp')), may hold values from -1.5 to 4.8, as said below
- bias_up: float32 [3072], P(('dp', 'fsdp')), may hold values from -1.5 to 1.5
- row_qkv: float32 [768], P(('dp', 'fsdp')), may hold values from 6553.6 to 24576
- col_qkv: float32 [2304], replicated, may hold values from 6553.6 to 13107.2
- row_out: float32 [768], P(('dp', 'fsdp')), may hold values from 819.2 to 3276.8
- col_out: float32 [768], replicated, may hold values from 819.2 to 3276.8
- row_up: float32 [768], P(('dp', 'fsdp')), may hold values from 983.04 to 3604.48
- col_up: float32 [3072], replicated, may hold values from 983.04 to 1966.08
- row_down: float32 [3072], P(('dp', 'fsdp')), may hold values from 3604.48 to 14745.6
- col_down: float32 [768], replicated, may hold values from 3604.48 to 14745.6
- moment_vectors: float32 [768, 8], P(('dp', 'fsdp')), may hold values from 1638.4 to 16384
- moment_bias_up: float32 [3072], P(('dp', 'fsdp')), may hold values from 819.2 to 3276.8
Outputs:
- out_tokens: bfloat16 [32768, 768], P(('dp', 'fsdp'))
- pooled: float32 [32, 24, 768], P(('dp', 'fsdp'))
- grad_tokens: float32 [32768, 768], P(('dp', 'fsdp'))
- grad_w_qkv: float32 [768, 2304], P(('dp', 'fsdp'))
- new_row_qkv: float32 [768], P(('dp', 'fsdp'))
- new_col_qkv: float32 [2304], replicated
- new_w_qkv: float32 [768, 2304], P(('dp', 'fsdp'))
- grad_w_out: float32 [768, 768], P(('dp', 'fsdp'))
- new_row_out: float32 [768], P(('dp', 'fsdp'))
- new_col_out: float32 [768], replicated
- new_w_out: float32 [768, 768], P(('dp', 'fsdp'))
- grad_w_up: float32 [768, 3072], P(('dp', 'fsdp'))
- new_row_up: float32 [768], P(('dp', 'fsdp'))
- new_col_up: float32 [3072], replicated
- new_w_up: float32 [768, 3072], P(('dp', 'fsdp'))
- grad_w_down: float32 [3072, 768], P(('dp', 'fsdp'))
- new_row_down: float32 [3072], P(('dp', 'fsdp'))
- new_col_down: float32 [768], replicated
- new_w_down: float32 [3072, 768], P(('dp', 'fsdp'))
- grad_vectors: float32 [768, 8], P(('dp', 'fsdp'))
- new_moment_vectors: float32 [768, 8], P(('dp', 'fsdp'))
- new_vectors: float32 [768, 8], P(('dp', 'fsdp'))
- grad_bias_up: float32 [3072], P(('dp', 'fsdp'))
- new_moment_bias_up: float32 [3072], P(('dp', 'fsdp'))
- new_bias_up: float32 [3072], P(('dp', 'fsdp'))
- clip_scale: float32 [], replicated
The draws below stay inside these ranges and needn't reach their ends.
Inputs may be any that keep to these rules, and one draw needn't show every extreme that they name: ends[r, s] is the last position of caption s of row r: they rise strictly along s, the last of each row is 1023, and each caption holds between 21 and 64 positions. `vectors`: columns 0 and 2 (the norms' gains) are positive; the other columns are biases of both signs.
All inputs are finite; a program needn't handle non-finite values.
Results may differ from the reference program's by a relative error of at most 0.01.
The reference program's roundings to bfloat16 on the way count: a program that leaves them out, or rounds other values in their place, can miss the bound.
Values may be sent and summed in bfloat16 or wider, within the bound.
A program may use at most 256 MiB of HBM per device.

```python
import math
import jax
import jax.numpy as jnp
from jax import lax

D = 768
HEADS = 12
HEAD_DIM = 64
FF = 3072
SEQ = 1024
SEGS = 24
STEP = 10
ROWS = 32
TOKENS = 32768


def draw_ends(key, part):
    key = jax.random.fold_in(key, 11)
    base_len = SEQ // SEGS
    spare = SEQ % SEGS
    half_len = base_len // 2

    def one_row(row_key):
        perm_key, delta_key = jax.random.split(row_key)
        order = jax.random.permutation(perm_key, SEGS)
        deltas = jax.random.randint(delta_key, (SEGS // 2,), -half_len, half_len + 1)
        deltas = deltas.at[0].set(half_len)
        lengths = base_len + (jnp.arange(SEGS) < spare).astype(jnp.int32)
        lengths = lengths.at[order[0::2]].add(deltas).at[order[1::2]].add(-deltas)
        return jnp.cumsum(lengths) - 1
    row_keys = jax.random.split(key, ROWS)
    return jax.vmap(one_row)(row_keys).astype(jnp.int32)


def draw_vectors(key, part):
    key = jax.random.fold_in(key, 7)
    rough_key, shift_key = jax.random.split(key)
    ramp = jnp.linspace(0.0, 1.0, D, dtype=jnp.float32)[:, None]
    rough = jax.random.uniform(rough_key, (D, 8), jnp.float32, 0.8, 1.2)
    gains = 0.3 * jnp.exp(2.3025851 * ramp) * rough
    shifts = jnp.clip(0.3 * jax.random.normal(shift_key, (D, 8), jnp.float32), -1.5, 1.5)
    columns = jnp.arange(8)
    is_gain = (columns == 0) | (columns == 2)
    return jnp.where(is_gain[None, :], gains, shifts).astype(jnp.float32)


def steps_of(key, dims, shards, smallest, largest):
    def one(dim, blocks):
        heights = jax.random.uniform(jax.random.fold_in(jax.random.fold_in(key, 6), dim), (blocks,), jnp.float32, smallest / len(shards), largest / len(shards))
        return jnp.repeat(jnp.exp(heights), dims[dim] // blocks).reshape((-1,) + (1,) * (len(dims) - dim - 1))

    level = one(*shards[0])
    for cut in shards[1:]:
        level = level * one(*cut)
    return level


def bell_draw(own_key, extent, width, limit, pieces=(), held_as=jnp.bfloat16):
    array = width * jax.random.normal(own_key, extent, jnp.float32)
    if pieces:
        array = array * steps_of(own_key, extent, pieces, -0.22, 0.18)
    return jnp.clip(array, -limit, limit).astype(held_as)


def setup_inputs(seed: int = 0) -> dict:
    key_list = jax.random.split(jax.random.key(seed), 21)
    tokens = bell_draw(key_list[0], (TOKENS, D), 1.0, 6.0, ((0, 32),))
    ends = draw_ends(jax.random.fold_in(key_list[20], 71), 0)
    cot_out = bell_draw(key_list[2], (TOKENS, D), 1.0, 6.0, ((0, 32),))
    cot_pooled = bell_draw(key_list[3], (ROWS, SEGS, D), 1.0, 6.0, ((0, 32),), jnp.float32)
    w_qkv = bell_draw(key_list[4], (D, 3 * D), D ** -0.5, 0.21875, ((0, 32),), jnp.float32)
    w_out = bell_draw(key_list[5], (D, D), (D // 32) ** -0.5, 1.25, ((0, 32),), jnp.float32)
    w_up = bell_draw(key_list[6], (D, FF), D ** -0.5, 0.21875, ((0, 32),), jnp.float32)
    w_down = bell_draw(key_list[7], (FF, D), FF ** -0.5, 0.109375, ((0, 32),), jnp.float32)
    vectors = draw_vectors(jax.random.fold_in(key_list[20], 71), 0)
    bias_up = bell_draw(key_list[9], (FF,), 0.3, 1.5, ((0, 32),), jnp.float32)
    row_qkv = jnp.clip(jnp.exp(math.log(24576.0) - 1.3217558 * jax.random.uniform(key_list[10], (D,), jnp.float32) ** steps_of(key_list[10], (D,), ((0, 32),), -0.2, 0.2)), 6553.6, 24576.0)
    col_qkv = jnp.clip(jnp.exp(jax.random.uniform(key_list[11], (3 * D,), jnp.float32, math.log(6553.6), math.log(13107.2))), 6553.6, 13107.2)
    row_out = jnp.clip(jnp.exp(math.log(3276.8) - 1.3862944 * jax.random.uniform(key_list[12], (D,), jnp.float32) ** steps_of(key_list[12], (D,), ((0, 32),), -0.2, 0.2)), 819.2, 3276.8)
    col_out = jnp.clip(jnp.exp(jax.random.uniform(key_list[13], (D,), jnp.float32, math.log(819.2), math.log(3276.8))), 819.2, 3276.8)
    row_up = jnp.clip(jnp.exp(math.log(3604.48) - 1.299283 * jax.random.uniform(key_list[14], (D,), jnp.float32) ** steps_of(key_list[14], (D,), ((0, 32),), -0.2, 0.2)), 983.04, 3604.48)
    col_up = jnp.clip(jnp.exp(jax.random.uniform(key_list[15], (FF,), jnp.float32, math.log(983.04), math.log(1966.08))), 983.04, 1966.08)
    row_down = jnp.clip(jnp.exp(math.log(14745.6) - 1.4087672 * jax.random.uniform(key_list[16], (FF,), jnp.float32) ** steps_of(key_list[16], (FF,), ((0, 32),), -0.2, 0.2)), 3604.48, 14745.6)
    col_down = jnp.clip(jnp.exp(jax.random.uniform(key_list[17], (D,), jnp.float32, math.log(3604.48), math.log(14745.6))), 3604.48, 14745.6)
    moment_vectors = jnp.clip(jnp.exp(math.log(16384.0) - 2.3025851 * jax.random.uniform(key_list[18], (D, 8), jnp.float32) ** steps_of(key_list[18], (D, 8), ((0, 32),), -0.2, 0.2)), 1638.4, 16384.0)
    moment_bias_up = jnp.clip(jnp.exp(math.log(3276.8) - 1.3862944 * jax.random.uniform(key_list[19], (FF,), jnp.float32) ** steps_of(key_list[19], (FF,), ((0, 32),), -0.2, 0.2)), 819.2, 3276.8)
    return dict(tokens=tokens, ends=ends, cot_out=cot_out, cot_pooled=cot_pooled, w_qkv=w_qkv, w_out=w_out, w_up=w_up, w_down=w_down, vectors=vectors, bias_up=bias_up, row_qkv=row_qkv, col_qkv=col_qkv, row_out=row_out, col_out=col_out, row_up=row_up, col_up=col_up, row_down=row_down, col_down=col_down, moment_vectors=moment_vectors, moment_bias_up=moment_bias_up)


@jax.custom_vjp
def low(v):
    return lax.optimization_barrier(v.astype(jnp.bfloat16)).astype(jnp.float32)

@jax.custom_vjp
def low_back(v):
    return v

def low_keep(v):
    return (low(v), None)

def low_pass(kept, grad):
    return (grad,)

def back_keep(v):
    return (v, None)

def back_low(kept, grad):
    return (low(grad),)
low.defvjp(low_keep, low_pass)
low_back.defvjp(back_keep, back_low)
norm_eps = 1e-06
square_eps = 1e-30
clip_limit = 1.0
step_rate = 0.5
scale_floor = 0.001
highest = lax.Precision.HIGHEST

def layer_norm(values, gain, shift):
    centre = lax.optimization_barrier(jnp.mean(values, -1, keepdims=True))
    centred = values - centre
    spread = lax.optimization_barrier(jnp.mean(centred * centred, -1, keepdims=True))
    return centred * lax.rsqrt(spread + norm_eps) * gain + shift

def exact_dot(left, right):
    return jnp.dot(left, right, precision=highest, preferred_element_type=jnp.float32)

def attention(queries, keys, values, segment):
    length = queries.shape[0]
    block = min(512, length)
    count = length // block
    factor = HEAD_DIM ** (-0.5)
    key_heads = keys.reshape(length, HEADS, HEAD_DIM)
    value_heads = values.reshape(length, HEADS, HEAD_DIM)

    def one_block(entry):
        query_block, segment_block = entry
        raw = jnp.einsum('qhd,khd->hqk', query_block, key_heads, precision=highest)
        scores = low_back(raw * factor)
        same = segment_block[:, None] == segment[None, :]
        scores = jnp.where(same[None], scores, -1e+30)
        peak = lax.optimization_barrier(jnp.max(scores, -1, keepdims=True))
        expo = jnp.exp(scores - peak)
        probs = low(expo / lax.optimization_barrier(jnp.sum(expo, -1, keepdims=True)))
        return jnp.einsum('hqk,khd->qhd', probs, value_heads, precision=highest)
    blocks = lax.map(jax.checkpoint(one_block), (queries.reshape(count, block, HEADS, HEAD_DIM), segment.reshape(count, block)))
    return blocks.reshape(length, HEADS * HEAD_DIM)

def row_forward(inputs, ends_row, w_qkv, w_out, w_up, w_down, vectors, bias_up):
    places = jnp.arange(SEQ, dtype=jnp.int32)
    segment = lax.optimization_barrier(jnp.sum((places[:, None] > ends_row[None, :]).astype(jnp.int32), 1))
    normed_one = low(layer_norm(inputs, vectors[:, 0], vectors[:, 1]))
    projected = exact_dot(normed_one, w_qkv)
    queries = low(low_back(projected[:, :D] + vectors[:, 4]))
    keys = low(low_back(projected[:, D:2 * D]))
    values = low(low_back(projected[:, 2 * D:] + vectors[:, 5]))
    attended = low(low_back(attention(queries, keys, values, segment)))
    middle = inputs + low_back(exact_dot(attended, w_out) + vectors[:, 6])
    normed_two = low(layer_norm(middle, vectors[:, 2], vectors[:, 3]))
    hidden_pre = low_back(exact_dot(normed_two, w_up) + bias_up)
    hidden = low(jax.nn.gelu(hidden_pre, approximate=True))
    final = middle + low_back(exact_dot(hidden, w_down) + vectors[:, 7])
    picker = (places[None, :] == ends_row[:, None]).astype(jnp.float32)
    return (final, exact_dot(picker, final))

def reference(tokens, ends, cot_out, cot_pooled, w_qkv, w_out, w_up, w_down, vectors, bias_up, row_qkv, col_qkv, row_out, col_out, row_up, col_up, row_down, col_down, moment_vectors, moment_bias_up):
    masters = (w_qkv, w_out, w_up, w_down, vectors, bias_up)
    row_total = ends.shape[0]
    inputs = tokens.astype(jnp.float32).reshape(row_total, SEQ, D)
    cotangents = cot_out.astype(jnp.float32).reshape(row_total, SEQ, D)

    def one_row(sums, entry):
        input_row, ends_row, cot_row, pooled_cot = entry

        def forward(values, weights):
            rounded = tuple((low(weight) for weight in weights))
            return row_forward(values, ends_row, *rounded)
        (result, pooled_row), pull = jax.vjp(forward, input_row, masters)
        grad_input, grad_weights = pull((cot_row, pooled_cot))
        sums = tuple((total + part for total, part in zip(sums, grad_weights)))
        return (sums, (result.astype(jnp.bfloat16), pooled_row, grad_input))
    start_sums = tuple((jnp.zeros(weight.shape, jnp.float32) for weight in masters))
    summed, (results, pooled, grad_inputs) = lax.scan(one_row, start_sums, (inputs, ends, cotangents, cot_pooled))
    grad_qkv, grad_out, grad_up, grad_down, grad_vec, grad_upbias = summed
    decay = 1.0 - STEP ** (-0.8)

    def factored(grad, row_old, col_old):
        squares = grad * grad + square_eps
        row_new = decay * row_old + (1.0 - decay) * lax.optimization_barrier(jnp.mean(squares, 1))
        col_new = decay * col_old + (1.0 - decay) * lax.optimization_barrier(jnp.mean(squares, 0))
        update = grad * lax.rsqrt(row_new[:, None] * col_new[None, :] / jnp.mean(row_new))
        return (update, row_new, col_new)
    upd_qkv, nrow_qkv, ncol_qkv = factored(grad_qkv, row_qkv, col_qkv)
    upd_out, nrow_out, ncol_out = factored(grad_out, row_out, col_out)
    upd_up, nrow_up, ncol_up = factored(grad_up, row_up, col_up)
    upd_down, nrow_down, ncol_down = factored(grad_down, row_down, col_down)
    moment_vec = decay * moment_vectors + (1.0 - decay) * (grad_vec * grad_vec + square_eps)
    upd_vec = grad_vec * lax.rsqrt(moment_vec)
    moment_upb = decay * moment_bias_up + (1.0 - decay) * (grad_upbias * grad_upbias + square_eps)
    upd_upb = grad_upbias * lax.rsqrt(moment_upb)
    updates = (upd_qkv, upd_out, upd_up, upd_down, upd_vec, upd_upb)
    square_total = sum((jnp.sum(update * update) for update in updates))
    param_count = 4 * D * D + 2 * D * FF + 8 * D + FF
    clip = jnp.maximum(1.0, jnp.sqrt(square_total / param_count) / clip_limit)

    def renew(weight, update, scale):
        return weight - step_rate * scale * update / clip

    def tensor_scale(weight):
        return jnp.maximum(scale_floor, jnp.sqrt(jnp.mean(weight * weight)))
    new_qkv = renew(w_qkv, upd_qkv, tensor_scale(w_qkv))
    new_out = renew(w_out, upd_out, tensor_scale(w_out))
    new_up = renew(w_up, upd_up, tensor_scale(w_up))
    new_down = renew(w_down, upd_down, tensor_scale(w_down))
    vec_scale = jnp.maximum(scale_floor, jnp.sqrt(lax.optimization_barrier(jnp.mean(vectors * vectors, 0))))[None, :]
    new_vec = renew(vectors, upd_vec, vec_scale)
    new_upb = renew(bias_up, upd_upb, tensor_scale(bias_up))
    return (results.reshape(row_total * SEQ, D), pooled, grad_inputs.reshape(row_total * SEQ, D), grad_qkv, nrow_qkv, ncol_qkv, new_qkv, grad_out, nrow_out, ncol_out, new_out, grad_up, nrow_up, ncol_up, new_up, grad_down, nrow_down, ncol_down, new_down, grad_vec, moment_vec, new_vec, grad_upbias, moment_upb, new_upb, clip)
```

```python
import functools

import jax
import jax.numpy as jnp
from jax import lax
from jax.experimental import pallas as pl
from jax.experimental.pallas import tpu as pltpu
from jax.sharding import PartitionSpec as P

D = 768
HEADS = 12
HEAD_DIM = 64
FF = 3072
SEQ = 1024
STEP = 10
REACH = 64
QUERIES = 64
WINDOW = 192
GROUP = 4
WIDE = GROUP * HEAD_DIM

norm_eps = 1e-06
square_eps = 1e-30
clip_limit = 1.0
step_rate = 0.5
scale_floor = 0.001
decay = 1.0 - STEP ** (-0.8)

f32 = jnp.float32
bf16 = jnp.bfloat16
MESH = pl.DeviceIdType.MESH
VMEM_LIMIT = 60 * 1024 * 1024


def dot_nn(left, right):
    return jnp.dot(left, right, preferred_element_type=f32)


def dot_tn(left, right):
    return lax.dot_general(left, right, (((0,), (0,)), ((), ())), preferred_element_type=f32)


def dot_nt(left, right):
    return lax.dot_general(left, right, (((1,), (1,)), ((), ())), preferred_element_type=f32)


def span(index, size):
    return pl.ds(pl.multiple_of(index * size, size), size)


def columns(ref, index, size):
    cut = ref[(slice(None),) * (len(ref.shape) - 1) + (span(index, size),)]
    return cut.reshape(-1, size)


def normalise(values):
    centre = jnp.mean(values, -1, keepdims=True)
    centred = values - centre
    scale = lax.rsqrt(jnp.mean(centred * centred, -1, keepdims=True) + norm_eps)
    return centred * scale, scale


def normalise_back(grad, gain, unit, scale):
    inner = grad * gain
    along = jnp.mean(inner * unit, -1, keepdims=True)
    return scale * (inner - jnp.mean(inner, -1, keepdims=True) - unit * along)


def caption_bounds(ends, bounds):
    shape = (SEQ // QUERIES, GROUP * QUERIES)
    places = lax.broadcasted_iota(jnp.int32, shape, 0) * QUERIES
    places = places + lax.rem(lax.broadcasted_iota(jnp.int32, shape, 1), QUERIES)
    first = jnp.zeros(shape, jnp.int32)
    last = jnp.full(shape, SEQ - 1, jnp.int32)
    for index in range(ends.shape[1]):
        end = ends[0, index]
        first = jnp.where(places > end, jnp.maximum(first, end + 1), first)
        last = jnp.where(places <= end, jnp.minimum(last, end), last)
    bounds[0] = first
    bounds[1] = last


def tile_mask(bounds, tile, start):
    places = start + lax.broadcasted_iota(jnp.int32, (WINDOW, GROUP * QUERIES), 0)
    row = pl.ds(tile, 1)
    inside = (places >= bounds[0, row, :]) & (places <= bounds[1, row, :])
    return jnp.where(inside, 0.0, -1e30).astype(f32)


def window_start(tile):
    start = jnp.clip(tile * QUERIES - REACH, 0, SEQ - WINDOW)
    return pl.multiple_of(start, REACH)


def head_of(shape):
    return lax.broadcasted_iota(jnp.int32, shape, 1) // HEAD_DIM


def split_heads(rows):
    head, zero = head_of(rows.shape), jnp.zeros_like(rows)
    return jnp.concatenate([jnp.where(head == index, rows, zero) for index in range(GROUP)], 0)


def join_heads(blocks):
    shape = (blocks.shape[0] // GROUP, blocks.shape[1])
    head, result = head_of(shape), blocks[: shape[0]]
    for index in range(1, GROUP):
        result = jnp.where(head == index, blocks[index * shape[0] : (index + 1) * shape[0]], result)
    return result


def probabilities(keys, queries, mask):
    scores = dot_nt(keys, queries) + mask
    expo = jnp.exp(scores - jnp.max(scores, 0, keepdims=True))
    return expo * (1.0 / jnp.sum(expo, 0, keepdims=True))


def scaled(queries):
    return queries * jnp.asarray(HEAD_DIM ** (-0.5), queries.dtype)


def first_norm(tokens, vec, normed):
    def step(part, carry):
        rows = span(part, 256)
        unit, _ = normalise(tokens[rows, :].astype(f32))
        normed[rows, :] = (unit * vec[0:1, :] + vec[1:2, :]).astype(bf16)
        return carry

    lax.fori_loop(0, SEQ // 256, step, 0)


def project(normed, w_qkv, vec, proj):
    def step(part, carry):
        weight = columns(w_qkv, part, D)
        shift = jnp.where(part == 0, vec[4:5, :], jnp.where(part == 2, vec[5:6, :], 0.0))
        for half in range(2):
            rows = pl.ds(half * 512, 512)
            proj[rows, span(part, D)] = (dot_nn(normed[rows, :], weight) + shift).astype(bf16)
        return carry

    lax.fori_loop(0, 3, step, 0)


def attend_tile(tile, proj, bounds, mixed):
    start = window_start(tile)
    rows, window = span(tile, QUERIES), pl.ds(start, WINDOW)
    mask = tile_mask(bounds, tile, start)
    for at in range(0, D, WIDE):
        queries = split_heads(scaled(proj[rows, at : at + WIDE]))
        keys = proj[window, D + at : D + at + WIDE]
        values = proj[window, 2 * D + at : 2 * D + at + WIDE]
        probs = probabilities(keys, queries, mask).astype(bf16)
        mixed[rows, at : at + WIDE] = join_heads(dot_tn(probs, values)).astype(bf16)


def middle_part(part, tokens, mixed, w_out, vec, middle, normed):
    rows = span(part, 512)
    weight = w_out[...].reshape(D, D)
    value = tokens[rows, :].astype(f32) + (dot_nn(mixed[rows, :], weight) + vec[6:7, :])
    middle[rows, :] = value
    unit, _ = normalise(value)
    normed[rows, :] = (unit * vec[2:3, :] + vec[3:4, :]).astype(bf16)


def forward_kernel(tokens, ends, w_qkv, w_out, vec, normed, proj, mixed, middle, normed_two, bounds):
    first_norm(tokens, vec, normed)
    project(normed, w_qkv, vec, proj)
    caption_bounds(ends, bounds)

    def tile(index, carry):
        attend_tile(2 * index, proj, bounds, mixed)
        attend_tile(2 * index + 1, proj, bounds, mixed)
        return carry

    lax.fori_loop(0, SEQ // QUERIES // 2, tile, 0)

    def part(index, carry):
        middle_part(index, tokens, mixed, w_out, vec, middle, normed_two)
        return carry

    lax.fori_loop(0, SEQ // 512, part, 0)


def vmem(count):
    return [pl.BlockSpec(memory_space=pltpu.VMEM)] * count


SMEM = pl.BlockSpec(memory_space=pltpu.SMEM)


def forward_call(tokens, ends, w_qkv, w_out, vec):
    shape = jax.ShapeDtypeStruct
    return pl.pallas_call(
        forward_kernel,
        out_shape=(
            shape((SEQ, D), bf16),
            shape((SEQ, 3 * D), bf16),
            shape((SEQ, D), bf16),
            shape((SEQ, D), f32),
            shape((SEQ, D), bf16),
        ),
        in_specs=vmem(1) + [SMEM] + vmem(3),
        out_specs=tuple(vmem(5)),
        scratch_shapes=[pltpu.VMEM((2, SEQ // QUERIES, GROUP * QUERIES), jnp.int32)],
        compiler_params=pltpu.CompilerParams(vmem_limit_bytes=VMEM_LIMIT),
        name="forward",
    )(tokens, ends, w_qkv, w_out, vec)


def feed_kernel(
    normed,
    middle,
    w_up,
    w_down,
    vec,
    bias,
    cot_out,
    cot_pooled,
    ends,
    out,
    pooled,
    grad_middle,
    grad_up,
    grad_down,
    grad_small,
    final,
    grad_final,
    low_final,
    grad_normed,
    normed_t,
    hidden,
    grad_pre,
):
    wide, tall = D, 512
    grad_final[...] = cot_out[...].astype(f32)
    for index in range(ends.shape[1]):
        row = pl.ds(ends[0, index], 1)
        grad_final[row, :] = grad_final[row, :] + cot_pooled[0, index : index + 1, :]
    low_final[...] = grad_final[...].astype(bf16)
    grad_small[...] = jnp.zeros_like(grad_small)
    grad_small[7:8, :] = jnp.sum(low_final[...].astype(f32), 0, keepdims=True)
    final[...] = middle[...] + vec[7:8, :]
    grad_normed[...] = jnp.zeros_like(grad_normed)
    normed_t[...] = normed[...].T
    root = 0.7978845608028654
    cube = 0.044715

    def chunk(part, carry):
        place = span(part, wide)
        shift = bias[:, place]

        def rows_step(block, total):
            rows = span(block, tall)
            pre = dot_nn(normed[rows, :], w_up[:, place]) + shift
            square = pre * pre
            bend = jnp.tanh(root * (pre + cube * (square * pre)))
            half = 0.5 * (1.0 + bend)
            slope = half + 0.5 * pre * (1.0 - bend * bend) * (root + (3.0 * root * cube) * square)
            act = (pre * half).astype(bf16)
            hidden[rows, :] = act
            final[rows, :] = final[rows, :] + dot_nn(act, w_down[place, :])
            back = (dot_nt(low_final[rows, :], w_down[place, :]) * slope).astype(bf16)
            grad_pre[rows, :] = back
            grad_normed[rows, :] = grad_normed[rows, :] + dot_nt(back, w_up[:, place])
            return total + jnp.sum(back.astype(f32), 0, keepdims=True)

        total = lax.fori_loop(0, SEQ // tall, rows_step, jnp.zeros((1, wide), f32))
        grad_small[pl.ds(8 + part, 1), :] = total
        grad_down[place, :] = dot_tn(hidden[...], low_final[...]).astype(bf16)
        grad_up[:, place] = dot_nn(normed_t[...], grad_pre[...]).astype(bf16)
        return carry

    lax.fori_loop(0, FF // wide, chunk, 0)
    out[...] = final[...].astype(bf16)
    for index in range(ends.shape[1]):
        pooled[0, index : index + 1, :] = final[pl.ds(ends[0, index], 1), :]

    def back(part, carry):
        gain, shift = carry
        rows = span(part, 256)
        unit, scale = normalise(middle[rows, :])
        grad = grad_normed[rows, :]
        grad_middle[rows, :] = grad_final[rows, :] + normalise_back(grad, vec[2:3, :], unit, scale)
        return gain + jnp.sum(grad * unit, 0, keepdims=True), shift + jnp.sum(grad, 0, keepdims=True)

    zero = jnp.zeros((1, D), f32)
    gain, shift = lax.fori_loop(0, SEQ // 256, back, (zero, zero))
    grad_small[2:3, :] = gain
    grad_small[3:4, :] = shift


def feed_call(normed, middle, w_up, w_down, vec, bias, cot_out, cot_pooled, ends):
    shape = jax.ShapeDtypeStruct
    count = ends.shape[1]
    return pl.pallas_call(
        feed_kernel,
        out_shape=(
            shape((SEQ, D), bf16),
            shape((1, count, D), f32),
            shape((SEQ, D), f32),
            shape((D, FF), bf16),
            shape((FF, D), bf16),
            shape((16, D), f32),
        ),
        in_specs=vmem(8) + [SMEM],
        out_specs=tuple(vmem(6)),
        scratch_shapes=[
            pltpu.VMEM((SEQ, D), f32),
            pltpu.VMEM((SEQ, D), f32),
            pltpu.VMEM((SEQ, D), bf16),
            pltpu.VMEM((SEQ, D), f32),
            pltpu.VMEM((D, SEQ), bf16),
            pltpu.VMEM((SEQ, D), bf16),
            pltpu.VMEM((SEQ, D), bf16),
        ],
        compiler_params=pltpu.CompilerParams(vmem_limit_bytes=VMEM_LIMIT),
        name="feed_forward",
    )(normed, middle, w_up, w_down, vec, bias, cot_out, cot_pooled, ends)


def attend_tile_back(tile, proj, bounds, grad_mixed, grad_proj, grad_keys, grad_values):
    start = window_start(tile)
    rows, window = span(tile, QUERIES), pl.ds(start, WINDOW)
    mask = tile_mask(bounds, tile, start)
    for at in range(0, D, WIDE):
        here = slice(at, at + WIDE)
        queries = split_heads(scaled(proj[rows, here]))
        grads = split_heads(grad_mixed[rows, here])
        keys = proj[window, D + at : D + at + WIDE]
        values = proj[window, 2 * D + at : 2 * D + at + WIDE]
        probs = probabilities(keys, queries, mask)
        grad_probs = dot_nt(values, grads)
        along = jnp.sum(probs * grad_probs, 0, keepdims=True)
        grad_scores = (probs * (grad_probs - along)).astype(bf16)
        both = join_heads(dot_tn(grad_scores, keys)) * HEAD_DIM ** (-0.5)
        grad_proj[rows, here] = both.astype(bf16)
        grad_keys[window, here] += dot_nn(grad_scores, queries)
        grad_values[window, here] += dot_nn(probs.astype(bf16), grads)


def out_back_part(part, grad_middle, w_out, low_middle, grad_mixed, total):
    rows = span(part, 512)
    low = grad_middle[rows, :].astype(bf16)
    low_middle[rows, :] = low
    grad_mixed[rows, :] = dot_nt(low, w_out[...].reshape(D, D)).astype(bf16)
    return total + jnp.sum(low.astype(f32), 0, keepdims=True)


def finish_proj(grad_proj, grad_keys, grad_values, grad_small):
    grad_proj[:, D : 2 * D] = grad_keys[...].astype(bf16)
    grad_proj[:, 2 * D :] = grad_values[...].astype(bf16)
    grad_small[4:5, :] = jnp.sum(grad_proj[:, :D].astype(f32), 0, keepdims=True)
    grad_small[5:6, :] = jnp.sum(grad_proj[:, 2 * D :].astype(f32), 0, keepdims=True)


def project_back(normed_t, grad_proj, grad_qkv):
    def step(part, carry):
        place = span(part, D)
        grad_qkv[:, place] = dot_nn(normed_t[...], grad_proj[:, place]).astype(bf16)
        return carry

    lax.fori_loop(0, 3, step, 0)


def tokens_back(tokens, grad_proj, w_qkv, vec, grad_middle, grad_tokens, grad_small):
    def step(part, carry):
        gain, shift = carry
        rows = span(part, 512)
        grad = dot_nt(grad_proj[rows, :], w_qkv[...].reshape(D, 3 * D))
        unit, scale = normalise(tokens[rows, :].astype(f32))
        grad_tokens[rows, :] = grad_middle[rows, :] + normalise_back(grad, vec[0:1, :], unit, scale)
        return gain + jnp.sum(grad * unit, 0, keepdims=True), shift + jnp.sum(grad, 0, keepdims=True)

    zero = jnp.zeros((1, D), f32)
    gain, shift = lax.fori_loop(0, SEQ // 512, step, (zero, zero))
    grad_small[0:1, :] = gain
    grad_small[1:2, :] = shift


def backward_kernel(
    tokens,
    ends,
    w_qkv,
    w_out,
    vec,
    normed,
    proj,
    mixed,
    grad_middle,
    small,
    grad_tokens,
    grad_qkv,
    grad_out,
    grad_small,
    bounds,
    low_middle,
    grad_mixed,
    turned,
    grad_proj,
    grad_keys,
    grad_values,
):
    grad_small[...] = small[...]

    def part(index, total):
        return out_back_part(index, grad_middle, w_out, low_middle, grad_mixed, total)

    grad_small[6:7, :] = lax.fori_loop(0, SEQ // 512, part, jnp.zeros((1, D), f32))
    turned[...] = mixed[...].T
    grad_out[...] = dot_nn(turned[...], low_middle[...]).astype(bf16)
    caption_bounds(ends, bounds)
    grad_keys[...] = jnp.zeros_like(grad_keys)
    grad_values[...] = jnp.zeros_like(grad_values)

    def tile(index, carry):
        attend_tile_back(2 * index, proj, bounds, grad_mixed, grad_proj, grad_keys, grad_values)
        attend_tile_back(2 * index + 1, proj, bounds, grad_mixed, grad_proj, grad_keys, grad_values)
        return carry

    lax.fori_loop(0, SEQ // QUERIES // 2, tile, 0)
    finish_proj(grad_proj, grad_keys, grad_values, grad_small)
    turned[...] = normed[...].T
    project_back(turned, grad_proj, grad_qkv)
    tokens_back(tokens, grad_proj, w_qkv, vec, grad_middle, grad_tokens, grad_small)


def backward_call(tokens, ends, w_qkv, w_out, vec, normed, proj, mixed, grad_middle, small):
    shape = jax.ShapeDtypeStruct
    return pl.pallas_call(
        backward_kernel,
        out_shape=(
            shape((SEQ, D), f32),
            shape((D, 3 * D), bf16),
            shape((D, D), bf16),
            shape((16, D), f32),
        ),
        in_specs=vmem(1) + [SMEM] + vmem(8),
        out_specs=tuple(vmem(4)),
        scratch_shapes=[
            pltpu.VMEM((2, SEQ // QUERIES, GROUP * QUERIES), jnp.int32),
            pltpu.VMEM((SEQ, D), bf16),
            pltpu.VMEM((SEQ, D), bf16),
            pltpu.VMEM((D, SEQ), bf16),
            pltpu.VMEM((SEQ, 3 * D), bf16),
            pltpu.VMEM((SEQ, D), f32),
            pltpu.VMEM((SEQ, D), f32),
        ],
        compiler_params=pltpu.CompilerParams(vmem_limit_bytes=VMEM_LIMIT),
        name="backward",
    )(tokens, ends, w_qkv, w_out, vec, normed, proj, mixed, grad_middle, small)


class Place:
    def __init__(self, mesh_shape):
        line, face = mesh_shape["dp"] // 2, lax.axis_index("dp")
        cell = lax.axis_index("fsdp")
        self.line = line
        self.z, self.y = lax.div(face, 2), lax.rem(face, 2)
        self.x, self.c = lax.div(cell, 2), lax.rem(cell, 2)
        self.flat = face * 4 + cell
        self.fill()

    def fill(self):
        y, x, c = self.y, self.x, self.c
        self.near = (y + (1 - c) * (1 - 2 * y), x + c * (1 - 2 * x))
        self.far = (y + c * (1 - 2 * y), x + (1 - c) * (1 - 2 * x))
        self.cross = (1 - y, 1 - x)
        self.own = (y, x)

    def other(self):
        place = object.__new__(Place)
        place.line, place.z, place.y, place.x, place.c = self.line, self.z, self.y, self.x, 1 - self.c
        place.fill()
        return place

    def device(self, z, spot, c):
        return (z * 2 + spot[0], spot[1] * 2 + c)

    def sibling(self):
        return self.device(self.z, self.own, 1 - self.c)

    def along(self, step):
        return lax.rem(self.z + step, self.line)

    def peers(self):
        return [
            self.sibling(),
            self.device(self.z, self.near, self.c),
            self.device(self.z, self.far, self.c),
        ] + [self.device(self.along(step), self.own, self.c) for step in range(1, self.line)]


def greet(place):
    barrier = pltpu.get_barrier_semaphore()
    peers = place.peers()
    for peer in peers:
        pl.semaphore_signal(barrier, inc=1, device_id=peer, device_id_type=MESH)
    pl.semaphore_wait(barrier, len(peers))


def remote(source, target, send, recv, device):
    return pltpu.make_async_remote_copy(
        src_ref=source,
        dst_ref=target,
        send_sem=send,
        recv_sem=recv,
        device_id=device,
        device_id_type=MESH,
    )


def band(c, half):
    return pl.ds(pl.multiple_of(c * half, 128), half)


GATHER_SEMS = 20


class Gather:
    def __init__(self, place, shard, stage, whole, send, recv):
        self.place, self.shard, self.stage, self.whole = place, shard, stage, whole
        self.send, self.recv = send, recv
        self.rows, self.half = shard.shape[0], shard.shape[1] // 2

    def block(self, z, spot, c):
        return self.whole.at[z, spot[0], span(spot[1], 2 * self.rows), band(c, self.half)]

    def line(self, spot, c):
        return self.whole.at[:, spot[0], span(spot[1], 2 * self.rows), band(c, self.half)]

    def copy(self, ref, index, device, target=None):
        return remote(ref, ref if target is None else target, self.send.at[index], self.recv.at[index], device)

    def get(self, ref, index):
        self.copy(ref, index, self.place.sibling()).wait_recv()

    def swap_copy(self):
        p = self.place
        source = self.shard.at[:, band(1 - p.c, self.half)]
        return self.copy(source, 0, p.sibling(), self.stage.at[span(p.c, self.rows), :])

    def own_copies(self):
        p = self.place
        block = self.block(p.z, p.own, p.c)
        return [self.copy(block, step, p.device(p.along(step), p.own, p.c)) for step in range(1, p.line)]

    def on_copies(self):
        p = self.place
        ref = self.line(p.own, p.c)
        return [
            self.copy(ref, p.line, p.device(p.z, p.near, p.c)),
            self.copy(ref, p.line + 1, p.device(p.z, p.far, p.c)),
        ]

    def cross_copy(self):
        p = self.place
        return self.copy(self.line(p.near, p.c), p.line + 2, p.device(p.z, p.far, p.c))

    def hand_copy(self, group):
        p = self.place
        spot = (p.own, p.near, p.far, p.cross)[group]
        return self.copy(self.line(spot, p.c), p.line + 3 + group, p.sibling())

    def swap(self):
        p = self.place
        self.swap_copy().start()
        self.stage[span(p.c, self.rows), :] = self.shard[:, band(p.c, self.half)]

    def own(self):
        p = self.place
        self.get(self.stage.at[span(1 - p.c, self.rows), :], 0)
        self.whole[p.z, p.y, span(p.x, 2 * self.rows), band(p.c, self.half)] = self.stage[...].astype(bf16)
        for copy in self.own_copies():
            copy.start()

    def along_z(self):
        p = self.place
        for step in range(1, p.line):
            self.get(self.block(p.along(p.line - step), p.own, p.c), step)
        for copy in self.on_copies():
            copy.start()
        self.hand_copy(0).start()

    def from_near(self):
        p = self.place
        self.get(self.line(p.near, p.c), p.line)
        self.cross_copy().start()
        self.hand_copy(1).start()

    def from_far(self):
        p = self.place
        self.get(self.line(p.far, p.c), p.line + 1)
        self.hand_copy(2).start()
        self.get(self.line(p.cross, p.c), p.line + 2)
        self.hand_copy(3).start()

    def finish(self):
        o = self.place.other()
        for group, spot in enumerate((o.own, o.near, o.far, o.cross)):
            self.get(self.line(spot, o.c), o.line + 3 + group)

    def drain(self):
        self.swap_copy().wait_send()
        for copy in self.own_copies() + self.on_copies():
            copy.wait_send()
        self.cross_copy().wait_send()
        for group in range(4):
            self.hand_copy(group).wait_send()


class GatherPlanes(Gather):
    def pair(self, pair, spot, c):
        return self.whole.at[2 * pair : 2 * pair + 2, spot[0], span(spot[1], 2 * self.rows), band(c, self.half)]

    def on_copies(self, pair):
        p = self.place
        ref, index = self.pair(pair, p.own, p.c), p.line + 4 * pair
        return [
            self.copy(ref, index, p.device(p.z, p.near, p.c)),
            self.copy(ref, index + 1, p.device(p.z, p.far, p.c)),
        ]

    def cross_copy(self, pair):
        p = self.place
        return self.copy(self.pair(pair, p.near, p.c), p.line + 4 * pair + 2, p.device(p.z, p.far, p.c))

    def hand_copy(self, pair):
        p = self.place
        ref = self.whole.at[2 * pair : 2 * pair + 2, :, :, band(p.c, self.half)]
        return self.copy(ref, p.line + 4 * pair + 3, p.sibling())

    def along_z(self, pair):
        p = self.place
        for plane in (2 * pair, 2 * pair + 1):
            step = lax.rem(p.z - plane + p.line, p.line)

            @pl.when(step != 0)
            def _():
                self.get(self.block(plane, p.own, p.c), step)

        for copy in self.on_copies(pair):
            copy.start()

    def from_near(self, pair):
        p = self.place
        self.get(self.pair(pair, p.near, p.c), p.line + 4 * pair)
        self.cross_copy(pair).start()

    def from_far(self, pair):
        p = self.place
        self.get(self.pair(pair, p.far, p.c), p.line + 4 * pair + 1)
        self.get(self.pair(pair, p.cross, p.c), p.line + 4 * pair + 2)
        self.hand_copy(pair).start()

    def finish(self, pair):
        ref = self.whole.at[2 * pair : 2 * pair + 2, :, :, band(1 - self.place.c, self.half)]
        self.get(ref, self.place.line + 4 * pair + 3)

    def drain(self):
        self.swap_copy().wait_send()
        for copy in self.own_copies():
            copy.wait_send()
        for pair in range(self.place.line // 2):
            for copy in self.on_copies(pair):
                copy.wait_send()
            self.cross_copy(pair).wait_send()
            self.hand_copy(pair).wait_send()


class Spread:
    def __init__(self, place, tiles, send, recv):
        self.place, self.tiles, self.send, self.recv = place, tiles, send, recv

    def copy(self, ref, index, device):
        return remote(ref, ref, self.send.at[index], self.recv.at[index], device)

    def get(self, ref, index):
        self.copy(ref, index, self.place.sibling()).wait_recv()

    def chips(self, spot):
        return self.tiles.at[:, spot[0], spot[1]]

    def copies(self, stage):
        p = self.place
        far = p.device(p.z, p.far, p.c)
        if stage == 0:
            return [self.copy(self.tiles.at[p.z, p.y, p.x, p.c], 0, p.sibling())]
        if stage == 1:
            chip = self.tiles.at[p.z, p.y, p.x]
            return [self.copy(chip, step, p.device(p.along(step), p.own, p.c)) for step in range(1, p.line)]
        if stage == 2:
            return [
                self.copy(self.chips(p.own), p.line, p.device(p.z, p.near, p.c)),
                self.copy(self.chips(p.own), p.line + 1, far),
            ]
        return [self.copy(self.chips(p.near), p.line + 2, far)]

    def start(self, stage):
        for copy in self.copies(stage):
            copy.start()

    def first(self):
        self.start(0)

    def second(self):
        p = self.place
        self.get(self.tiles.at[p.z, p.y, p.x, 1 - p.c], 0)
        self.start(1)

    def third(self):
        p = self.place
        for step in range(1, p.line):
            self.get(self.tiles.at[p.along(p.line - step), p.y, p.x], step)
        self.start(2)

    def fourth(self):
        p = self.place
        self.get(self.chips(p.near), p.line)
        self.start(3)

    def finish(self):
        p = self.place
        self.get(self.chips(p.far), p.line + 1)
        self.get(self.chips(p.cross), p.line + 2)

    def drain(self):
        for stage in range(4):
            for copy in self.copies(stage):
                copy.wait_send()


def fill_tiles(place, tiles, olds, vectors, bias, moment_vec, moment_bias):
    here = (place.z, place.y, place.x, place.c)
    tiles[here] = jnp.zeros(tiles.shape[4:], tiles.dtype)
    tile = jnp.zeros(olds.shape[4:], f32)
    olds[here] = tile
    olds[here + (slice(0, 8), slice(0, vectors.shape[1]))] = vectors[...]
    olds[here + (slice(8, 9), slice(0, bias.shape[1]))] = bias[...]
    tiles[here] = olds[here].astype(tiles.dtype)
    olds[here] = tile
    olds[here + (slice(0, 8), slice(0, vectors.shape[1]))] = moment_vec[...]
    olds[here + (slice(8, 9), slice(0, bias.shape[1]))] = moment_bias[...]


def lay_out(tiles, first, size, out):
    lane = lax.broadcasted_iota(jnp.int32, (8, 128), 1)
    done = [jnp.zeros((8, 128), f32) for _ in range(out.shape[1] // 128)]
    line, count = tiles.shape[0], tiles.shape[0] * 8
    for index in range(count):
        tile = tiles[index // 8, index // 4 % 2, index // 2 % 2, index % 2].astype(f32)[first : first + 8]
        at, shift = divmod(index * size, 128)
        turned = pltpu.roll(tile, shift, 1) if shift else tile
        done[at] = jnp.where((lane >= shift) & (lane < shift + size), turned, done[at])
        if shift + size > 128:
            done[at + 1] = jnp.where(lane < shift + size - 128, turned, done[at + 1])
    for index, tile in enumerate(done):
        out[:, index * 128 : index * 128 + 128] = tile[: out.shape[0]]


class Reduce:
    def __init__(self, place, terms, other, far, got_far, near, got_near, line, got_line, whole, result, send, recv, mine=None):
        self.place, self.terms, self.other, self.mine = place, terms, other, mine
        self.far, self.got_far, self.near, self.got_near = far, got_far, near, got_near
        self.line, self.got_line, self.whole, self.result = line, got_line, whole, result
        self.send, self.recv = send, recv
        self.half = other.shape[-1]
        self.rows = whole.shape[0] // 2

    def copy(self, source, target, index, device):
        return remote(source, target, self.send.at[index], self.recv.at[index], device)

    def get(self, ref, index):
        self.copy(ref, ref, index, self.place.sibling()).wait_recv()

    def swap_copy(self):
        p = self.place
        return self.copy(self.terms.at[:, :, :, band(1 - p.c, self.half)], self.other, 0, p.sibling())

    def far_copy(self, group):
        p = self.place
        return self.copy(self.far.at[group], self.got_far.at[group], 1 + group, p.device(p.z, p.far, p.c))

    def near_copy(self):
        p = self.place
        return self.copy(self.near, self.got_near, 3, p.device(p.z, p.near, p.c))

    def line_copy(self, step):
        p = self.place
        target = p.device(p.along(step), p.own, p.c)
        return self.copy(self.line.at[step - 1], self.got_line.at[step - 1], 3 + step, target)

    def owner_copy(self):
        p = self.place
        source = self.whole.at[span(1 - p.c, self.rows), :]
        return self.copy(source, self.result.at[:, band(p.c, self.half)], 3 + p.line, p.sibling())

    def mine_copy(self):
        p = self.place
        source = self.terms.at[:, :, :, band(p.c, self.half)]
        return pltpu.make_async_copy(source, self.mine, self.send.at[4 + p.line])

    def swap(self):
        self.swap_copy().start()
        if self.mine is not None:
            self.mine_copy().start()

    def meet(self):
        self.get(self.other, 0)
        if self.mine is not None:
            self.mine_copy().wait()

    def pair(self, z, spot):
        rows = span(spot[1], 2 * self.rows)
        if self.mine is None:
            mine = self.terms[z, spot[0], rows, band(self.place.c, self.half)]
        else:
            mine = self.mine[z, spot[0], rows, :]
        return mine.astype(f32) + self.other[z, spot[0], rows, :].astype(f32)

    def to_far(self):
        p = self.place
        self.meet()
        for group, spot in enumerate((p.cross, p.far)):
            for z in range(p.line):
                self.far[group, z] = self.pair(z, spot).astype(bf16)
            self.far_copy(group).start()

    def to_near(self):
        p = self.place
        self.get(self.got_far.at[0], 1)
        for z in range(p.line):
            self.near[z] = (self.pair(z, p.near) + self.got_far[0, z].astype(f32)).astype(bf16)
        self.near_copy().start()

    def sum_own(self, z):
        return self.pair(z, self.place.own) + self.got_far[1, z].astype(f32) + self.got_near[z].astype(f32)

    def to_line(self):
        p = self.place
        self.get(self.got_far.at[1], 2)
        self.get(self.got_near, 3)
        self.send_line()

    def send_line(self):
        p = self.place
        for step in range(1, p.line):
            self.line[step - 1] = self.sum_own(p.along(step)).astype(bf16)
            self.line_copy(step).start()
        self.whole[...] = self.sum_own(p.z)

    def to_owner(self):
        p = self.place
        total = self.whole[...]
        for step in range(1, p.line):
            self.get(self.got_line.at[step - 1], 3 + step)
            total = total + self.got_line[step - 1].astype(f32)
        self.whole[...] = total
        self.owner_copy().start()
        self.result[:, band(p.c, self.half)] = self.whole[span(p.c, self.rows), :]

    def finish(self):
        p = self.place
        self.get(self.result.at[:, band(1 - p.c, self.half)], 3 + p.line)

    def drain(self):
        p = self.place
        self.swap_copy().wait_send()
        for group in range(2):
            self.far_copy(group).wait_send()
        self.near_copy().wait_send()
        for step in range(1, p.line):
            self.line_copy(step).wait_send()
        self.owner_copy().wait_send()


class ReducePlanes:
    def __init__(self, place, first, terms, other, far, got_far, near, got_near, line, got_line, whole, result, send, recv, mine=None):
        self.place, self.first, self.terms, self.other, self.mine = place, first, terms, other, mine
        self.far, self.got_far, self.near, self.got_near = far, got_far, near, got_near
        self.line, self.got_line, self.whole, self.result = line, got_line, whole, result
        self.send, self.recv = send, recv
        self.half = other.shape[-1]
        self.plane = first + place.c

    def copy(self, source, target, index, device):
        return remote(source, target, self.send.at[index], self.recv.at[index], device)

    def get(self, ref, index):
        self.copy(ref, ref, index, self.place.sibling()).wait_recv()

    def swap_copy(self):
        p = self.place
        return self.copy(self.terms.at[:, :, :, band(1 - p.c, self.half)], self.other, 0, p.sibling())

    def far_copy(self, group):
        p = self.place
        return self.copy(self.far.at[group], self.got_far.at[group], 1 + group, p.device(p.z, p.far, p.c))

    def near_copy(self):
        p = self.place
        return self.copy(self.near, self.got_near, 3, p.device(p.z, p.near, p.c))

    def line_copy(self):
        p = self.place
        step = lax.rem(self.plane - p.z + p.line, p.line)
        return self.copy(self.line, self.got_line.at[step - 1], 3 + step, p.device(self.plane, p.own, p.c))

    def owner_copy(self):
        p = self.place
        return self.copy(self.whole.at[1 - p.c], self.result, 3 + p.line, p.sibling())

    def mine_copy(self):
        p = self.place
        source = self.terms.at[:, :, :, band(p.c, self.half)]
        return pltpu.make_async_copy(source, self.mine, self.send.at[4 + p.line])

    def swap(self):
        self.swap_copy().start()
        if self.mine is not None:
            self.mine_copy().start()

    def meet(self):
        self.get(self.other, 0)
        if self.mine is not None:
            self.mine_copy().wait()

    def pair(self, spot):
        chip = spot[0] * 2 + spot[1]
        mine = self.terms[chip, :, :, band(self.place.c, self.half)] if self.mine is None else self.mine[chip]
        return mine.astype(f32) + self.other[chip].astype(f32)

    def to_far(self):
        p = self.place
        self.meet()
        for group, spot in enumerate((p.cross, p.far)):
            self.far[group] = self.pair(spot).astype(bf16)
            self.far_copy(group).start()

    def to_near(self):
        self.get(self.got_far.at[0], 1)
        self.near[...] = (self.pair(self.place.near) + self.got_far[0].astype(f32)).astype(bf16)
        self.near_copy().start()

    def to_line(self):
        p = self.place
        self.get(self.got_far.at[1], 2)
        self.get(self.got_near, 3)
        self.send_line(self.pair(p.own) + self.got_far[1].astype(f32) + self.got_near[...].astype(f32))

    def send_line(self, own):
        p = self.place

        @pl.when(p.z == self.plane)
        def _():
            self.whole[...] = own

        @pl.when(p.z != self.plane)
        def _():
            self.line[...] = own.astype(bf16)
            self.line_copy().start()

    def to_owner(self):
        p = self.place

        @pl.when(p.z == self.plane)
        def _():
            total = self.whole[...]
            for step in range(1, p.line):
                self.get(self.got_line.at[step - 1], 3 + step)
                total = total + self.got_line[step - 1].astype(f32)
            self.whole[...] = total
            self.owner_copy().start()
            self.result[...] = self.whole[p.c]

    def finish(self):
        p = self.place

        @pl.when(p.z == self.first + 1 - p.c)
        def _():
            self.get(self.result, 3 + p.line)

    def drain(self):
        p = self.place
        self.swap_copy().wait_send()
        for group in range(2):
            self.far_copy(group).wait_send()
        self.near_copy().wait_send()
        self.drain_line()

    def drain_line(self):
        p = self.place

        @pl.when(p.z == self.plane)
        def _():
            self.owner_copy().wait_send()

        @pl.when(p.z != self.plane)
        def _():
            self.line_copy().wait_send()


class ReduceStart(Reduce):
    def __init__(self, place, terms, other, far, got_far, near, own, send, recv):
        self.place, self.terms, self.other, self.mine = place, terms, other, None
        self.far, self.got_far, self.near, self.own = far, got_far, near, own
        self.send, self.recv = send, recv
        self.half = other.shape[-1]
        self.rows = own.shape[1] // 2

    def pass_sum(self):
        p = self.place
        self.get(self.got_far.at[0], 1)
        self.get(self.got_far.at[1], 2)
        for z in range(p.line):
            self.near[z] = (self.pair(z, p.near) + self.got_far[0, z].astype(f32)).astype(bf16)
            self.own[z] = self.pair(z, p.own) + self.got_far[1, z].astype(f32)

    def drain(self):
        self.swap_copy().wait_send()
        for group in range(2):
            self.far_copy(group).wait_send()


class ReducePlanesStart(ReducePlanes):
    def __init__(self, place, terms, other, far, got_far, near, own, send, recv):
        self.place, self.terms, self.other, self.mine = place, terms, other, None
        self.far, self.got_far, self.near, self.own = far, got_far, near, own
        self.send, self.recv = send, recv
        self.half = other.shape[-1]

    def pass_sum(self):
        p = self.place
        self.get(self.got_far.at[0], 1)
        self.get(self.got_far.at[1], 2)
        self.near[...] = (self.pair(p.near) + self.got_far[0].astype(f32)).astype(bf16)
        self.own[...] = self.pair(p.own) + self.got_far[1].astype(f32)

    def drain(self):
        self.swap_copy().wait_send()
        for group in range(2):
            self.far_copy(group).wait_send()


class ReduceRest(Reduce):
    def __init__(self, place, near, own, got_near, line, got_line, whole, result, send, recv):
        self.place, self.near, self.own, self.got_near = place, near, own, got_near
        self.line, self.got_line, self.whole, self.result = line, got_line, whole, result
        self.send, self.recv = send, recv
        self.half = near.shape[-1]
        self.rows = whole.shape[0] // 2

    def to_near(self):
        self.near_copy().start()

    def sum_own(self, z):
        return self.own[z] + self.got_near[z].astype(f32)

    def to_line(self):
        p = self.place
        self.get(self.got_near, 3)
        self.send_line()

    def drain(self):
        p = self.place
        self.near_copy().wait_send()
        for step in range(1, p.line):
            self.line_copy(step).wait_send()
        self.owner_copy().wait_send()


class ReducePlanesRest(ReducePlanes):
    def __init__(self, place, first, near, own, got_near, line, got_line, whole, result, send, recv):
        self.place, self.first, self.near, self.own, self.got_near = place, first, near, own, got_near
        self.line, self.got_line, self.whole, self.result = line, got_line, whole, result
        self.send, self.recv = send, recv
        self.half = near.shape[-1]
        self.plane = first + place.c

    def to_near(self):
        self.near_copy().start()

    def to_line(self):
        self.get(self.got_near, 3)
        self.send_line(self.own[...] + self.got_near[...].astype(f32))

    def drain(self):
        self.near_copy().wait_send()
        self.drain_line()


def reduce_scratch(line, rows, half, count):
    return [
        pltpu.VMEM((count, line, 2, 2 * rows, half), bf16),
        pltpu.VMEM((count, 2, line, rows, half), bf16),
        pltpu.VMEM((count, 2, line, rows, half), bf16),
        pltpu.VMEM((count, line, rows, half), bf16),
        pltpu.VMEM((count, line, rows, half), bf16),
        pltpu.VMEM((count, line - 1, rows, half), bf16),
        pltpu.VMEM((count, line - 1, rows, half), bf16),
        pltpu.VMEM((count, rows, half), f32),
    ]


def plane_scratch(line, rows, half, count):
    block = (2, rows, half)
    return [
        pltpu.VMEM((count, 4) + block, bf16),
        pltpu.VMEM((count, 2) + block, bf16),
        pltpu.VMEM((count, 2) + block, bf16),
        pltpu.VMEM((count,) + block, bf16),
        pltpu.VMEM((count,) + block, bf16),
        pltpu.VMEM((count,) + block, bf16),
        pltpu.VMEM((count, line - 1) + block, bf16),
        pltpu.VMEM((count,) + block, f32),
    ]


class AllSum:
    def __init__(self, place, value, slots, line, send, recv):
        self.place, self.value, self.slots, self.line = place, value, slots, line
        self.send, self.recv = send, recv

    def start(self, stage):
        p = self.place
        device = (p.sibling(), p.device(p.z, (p.y, 1 - p.x), p.c), p.device(p.z, (1 - p.y, p.x), p.c))[stage]
        self.copy = remote(self.value, self.slots.at[stage], self.send.at[stage], self.recv.at[stage], device)
        self.copy.start()

    def end(self, stage):
        self.copy.wait()
        self.value[...] = self.value[...] + self.slots[stage]

    def start_line(self):
        p = self.place
        self.line[p.z] = self.value[...]
        self.copies = [
            remote(self.line.at[p.z], self.line.at[p.z], self.send.at[2 + step], self.recv.at[2 + step],
                   p.device(p.along(step), p.own, p.c))
            for step in range(1, p.line)
        ]
        for copy in self.copies:
            copy.start()

    def end_line(self):
        p = self.place
        for step in range(1, p.line):
            ref = self.line.at[p.along(p.line - step)]
            remote(ref, ref, self.send.at[2 + step], self.recv.at[2 + step], p.sibling()).wait_recv()
        total = self.line[0]
        for z in range(1, p.line):
            total = total + self.line[z]
        self.value[...] = total
        for copy in self.copies:
            copy.wait_send()

    def next(self, stage):
        self.end(stage)
        if stage < 2:
            self.start(stage + 1)
        else:
            self.start_line()


def sum_scratch(line, rows):
    return [
        pltpu.VMEM((rows, D), f32),
        pltpu.VMEM((3, rows, D), f32),
        pltpu.VMEM((line, rows, D), f32),
        pltpu.SemaphoreType.DMA((2 + line,)),
        pltpu.SemaphoreType.DMA((2 + line,)),
    ]


def diagonal(size):
    return lax.broadcasted_iota(jnp.int32, (size, size), 0) == lax.broadcasted_iota(jnp.int32, (size, size), 1)


def to_column(row):
    return jnp.sum(jnp.where(diagonal(row.shape[1]), row, 0.0), 1, keepdims=True)


def to_row(column):
    return jnp.sum(jnp.where(diagonal(column.shape[0]), column, 0.0), 0, keepdims=True)


def total(values):
    return jnp.sum(jnp.sum(values, 1, keepdims=True), 0, keepdims=True)


def own_vectors(place, small, size):
    shape = (size, D)
    pick = lax.broadcasted_iota(jnp.int32, shape, 1) == place.flat * size + lax.broadcasted_iota(jnp.int32, shape, 0)
    row = lax.broadcasted_iota(jnp.int32, (8, size), 0)
    result = jnp.zeros((8, size), f32)
    for index in range(8):
        column = jnp.sum(jnp.where(pick, small[index : index + 1, :], 0.0), 1, keepdims=True)
        result = jnp.where(row == index, to_row(column), result)
    return result


def own_bias(place, small, size):
    per = D // size
    row, at = lax.div(place.flat, per), lax.rem(place.flat, per) * size
    shape = (FF // D, D)
    kept = lax.broadcasted_iota(jnp.int32, shape, 0) == row
    line = jnp.sum(jnp.where(kept, small[8 : 8 + FF // D, :], 0.0), 0, keepdims=True)
    shape = (size, D)
    pick = lax.broadcasted_iota(jnp.int32, shape, 1) == at + lax.broadcasted_iota(jnp.int32, shape, 0)
    return to_row(jnp.sum(jnp.where(pick, line, 0.0), 1, keepdims=True))


ROW_COUNTS = (D, D, D, FF)
SIZES = (3 * D * D, D * D, D * FF, FF * D)


def row_statistic(grad, old):
    mean = jnp.sum(grad * grad + square_eps, 1, keepdims=True) * (1.0 / grad.shape[1])
    return decay * to_column(old) + (1.0 - decay) * mean


def moment_of(grad, old):
    return decay * old + (1.0 - decay) * (grad * grad + square_eps)


def finish_kernel(*refs):
    refs = list(refs)

    def take(count):
        taken = refs[:count]
        del refs[:count]
        return taken

    large, grads, (grad_vec, grad_bias, stats), weights, (vectors, bias), rows, cols, (moment_vec, moment_bias) = (
        take(3), take(4), take(3), take(4), take(2), take(4), take(4), take(2)
    )
    out_large, out_grads, new_rows, new_cols, new_weights = take(3), take(4), take(4), take(4), take(4)
    out_vec, new_moment_vec, new_vec, out_bias, new_moment_bias, new_bias, clip_out = take(7)
    held, sems = take(3), take(1)[0]
    copies = []
    for index, count in enumerate((4, 1, 8)):
        size = held[index].shape[0] // count
        for part in range(count):
            piece, at = pl.ds(part * size, size), len(copies)
            copies.append(
                (
                    pltpu.make_async_copy(large[index].at[piece], held[index].at[piece], sems.at[0, at]),
                    pltpu.make_async_copy(held[index].at[piece], out_large[index].at[piece], sems.at[1, at]),
                )
            )
    for copy_in, _ in copies:
        copy_in.start()
    sums = stats[18:19, :]

    def one(index):
        return sums[:, index : index + 1]

    norm = one(17)
    at = 0
    col_rows, row_means = [], []
    for index in range(4):
        width = grads[index].shape[1]
        count = width // D
        sums_of = jnp.concatenate([stats[at + part : at + part + 1, :] for part in range(count)], 1)
        weighed = jnp.concatenate([stats[9 + at + part : 10 + at + part, :] for part in range(count)], 1)
        at += count
        col = decay * cols[index][...].reshape(1, width) + (1.0 - decay) * (sums_of * (1.0 / ROW_COUNTS[index]))
        new_cols[index][...] = col.reshape(width)
        col_rows.append(col)
        row_sum = decay * one(index) + (1.0 - decay) * (total(sums_of) * (1.0 / width))
        row_means.append(row_sum * (1.0 / ROW_COUNTS[index]))
        norm = norm + total(weighed / col) * row_means[index]
    for copy_in, copy_out in copies:
        copy_in.wait()
        copy_out.start()
    param_count = sum(SIZES) + 8 * D + FF
    clip = jnp.maximum(1.0, jnp.sqrt(norm * (1.0 / param_count)) * (1.0 / clip_limit))
    clip_out[...] = clip
    for index in range(4):
        grad = grads[index][...]
        out_grads[index][...] = grad
        row = row_statistic(grad, rows[index][...])
        new_rows[index][...] = to_row(row)
        scale = jnp.maximum(scale_floor, jnp.sqrt(one(4 + index) * (1.0 / SIZES[index])))
        update = grad * lax.rsqrt(row * col_rows[index] / row_means[index])
        new_weights[index][...] = weights[index][...] - (step_rate * scale / clip) * update
    lane = lax.broadcasted_iota(jnp.int32, (8, 1), 0)
    scale = jnp.zeros((8, 1), f32)
    for index in range(8):
        scale = jnp.where(lane == index, one(8 + index), scale)
    scale = jnp.maximum(scale_floor, jnp.sqrt(scale * (1.0 / D)))
    vec = grad_vec[...]
    moment = moment_of(vec, moment_vec[...])
    out_vec[...] = vec
    new_moment_vec[...] = moment
    new_vec[...] = vectors[...] - (step_rate * scale / clip) * (vec * lax.rsqrt(moment))
    scale = jnp.maximum(scale_floor, jnp.sqrt(one(16) * (1.0 / FF)))
    low = grad_bias[...]
    moment = moment_of(low, moment_bias[...])
    out_bias[...] = low
    new_moment_bias[...] = moment
    new_bias[...] = bias[...] - (step_rate * scale / clip) * (low * lax.rsqrt(moment))
    for _, copy_out in copies:
        copy_out.wait()


def finish_call(large, summed, weights, vectors, bias, rows, cols, moment_vec, moment_bias):
    shape = jax.ShapeDtypeStruct
    like = [shape(w.shape, f32) for w in weights]
    vec, low = shape(vectors.shape, f32), shape(bias.shape, f32)
    return pl.pallas_call(
        finish_kernel,
        out_shape=tuple(
            [shape(value.shape, value.dtype) for value in large]
            + like
            + [shape(r.shape, f32) for r in rows]
            + [shape(c.shape, f32) for c in cols]
            + like
            + [vec, vec, vec, low, low, low, shape((1, 1), f32)]
        ),
        in_specs=[pl.BlockSpec(memory_space=pl.ANY)] * 3 + vmem(23),
        out_specs=tuple([pl.BlockSpec(memory_space=pl.ANY)] * 3 + vmem(23)),
        scratch_shapes=[pltpu.VMEM(value.shape, value.dtype) for value in large] + [pltpu.SemaphoreType.DMA((2, 13))],
        compiler_params=pltpu.CompilerParams(vmem_limit_bytes=VMEM_LIMIT),
        name="finish",
    )(*large, *summed, *weights, vectors, bias, *rows, *cols, moment_vec, moment_bias)


def pooled_rows(ends, cot_pooled, parts):
    lane = lax.rem(lax.broadcasted_iota(jnp.int32, (1, 96), 1), 32)
    spot = jnp.full((1, 96), -1, jnp.int32)
    for index in range(ends.shape[1]):
        spot = jnp.where(lane == index, ends[0, index], spot)
    left = cot_pooled[0]
    parts[...] = jnp.zeros_like(parts)
    for index in range(3):
        low = left.astype(bf16)
        parts[32 * index : 32 * index + left.shape[0], :] = low
        left = left - low.astype(f32)
    return spot


def attend_group(tile, group, proj, masks, mixed):
    start = window_start(tile)
    rows, window, at = span(tile, QUERIES), pl.ds(start, WINDOW), group * D
    mask = masks[tile]
    queries = split_heads(scaled(proj[rows, at : at + WIDE]))
    keys = proj[window, at + WIDE : at + 2 * WIDE]
    values = proj[window, at + 2 * WIDE : at + D]
    probs = probabilities(keys, queries, mask).astype(bf16)
    return rows, join_heads(dot_tn(probs, values)).astype(bf16)


def feed_rows(rows, cols, normed, up, down, bias, low_final, hidden, grad_pre, final, grad_normed):
    root = 0.7978845608028654
    cube = 0.044715
    pre = dot_nn(normed[rows, :], up()) + bias[0:1, cols]
    square = pre * pre
    half = 0.5 + 0.5 * jnp.tanh(pre * (root + (root * cube) * square))
    act = pre * half
    slope = half + act * ((1.0 - half) * (2.0 * root + (6.0 * root * cube) * square))
    act = act.astype(bf16)
    hidden[rows, :] = act
    final[rows, :] = final[rows, :] + dot_nn(act, down())
    back = (dot_nt(low_final[rows, :], down()) * slope).astype(bf16)
    grad_pre[rows, :] = back
    grad_normed[rows, :] = grad_normed[rows, :] + dot_nt(back, up())
    return jnp.sum(back.astype(f32), 0, keepdims=True)


def front_kernel(mesh_shape, *refs):
    refs = list(refs)

    def take(count):
        taken = refs[:count]
        del refs[:count]
        return taken

    tokens, ends, cot_out, cot_pooled, w_qkv, w_out, w_up, w_down = take(8)
    vectors, bias, moment_vec, moment_bias = take(4)
    out_both, out_normed, out_proj, out_mixed, out_tokens, out_middle, out_up, out_down, out_masks = take(9)
    vec, moments, pooled, grad_small, near_up, own_up, near_down, own_down = take(8)
    shards, stage, stage_down, weights, all_down, tiles, olds, all_bias = take(8)
    normed, proj, mixed, middle, normed_two, final, grad_middle, grad_normed, normed_t = take(9)
    bounds, masks, parts = take(3)
    up_scratch, down_scratch = take(3), take(3)
    send, recv, sum_send, sum_recv, tile_send, tile_recv, old_send, old_recv, out_sems = take(9)

    place = Place(mesh_shape)
    line = place.line
    cut = (line, 2, D // (2 * line), D)
    copies = {}

    def leave(name, source, target):
        copies[name] = pltpu.make_async_copy(source, target, out_sems.at[len(copies)])
        copies[name].start()

    spread = Spread(place, tiles, tile_send, tile_recv)
    old_spread = Spread(place, olds, old_send, old_recv)

    def gather_of(index, first, last):
        whole, half = slice(first * D, last * D), slice(first * D // 2, last * D // 2)
        return Gather(
            place, shards.at[:, whole], stage.at[:, half], weights.at[:, :, :, whole], send.at[index], recv.at[index]
        )

    g0, g1, g2, u0, u1 = (gather_of(*given) for given in ((0, 0, 1), (1, 1, 2), (2, 2, 3), (3, 3, 6), (4, 6, 8)))
    down = GatherPlanes(place, w_down, stage_down, all_down, send.at[5], recv.at[5])

    def begin():
        fill_tiles(place, tiles, olds, vectors, bias, moment_vec, moment_bias)
        greet(place)

    def lay_qkv():
        for group in range(3):
            for part in range(3):
                at = group * D + part * WIDE
                shards[:, at : at + WIDE] = w_qkv[:, part * D + group * WIDE : part * D + (group + 1) * WIDE]

    def lay_rest():
        shards[:, 3 * D : 4 * D] = w_out[...]
        shards[:, 4 * D :] = w_up[...]

    def cotangent():
        spot = pooled_rows(ends, cot_pooled, parts)
        caption_bounds(ends, bounds)

        def mask_of(tile, carry):
            masks[tile] = tile_mask(bounds, tile, window_start(tile))
            return carry

        lax.fori_loop(0, SEQ // QUERIES, mask_of, 0)
        leave("masks", masks, out_masks)

        def rows_of(part, carry):
            rows = span(part, 256)
            place_of = part * 256 + lax.broadcasted_iota(jnp.int32, (256, 96), 0)
            picked = dot_nn(jnp.where(place_of == spot, 1.0, 0.0).astype(bf16), parts[...])
            grad_middle[rows, :] = cot_out[rows, :].astype(f32) + picked
            return carry

        lax.fori_loop(0, SEQ // 256, rows_of, 0)

    def norm_tokens():
        lay_out(tiles, 0, vectors.shape[1], vec)
        first_norm(tokens, vec, normed)
        leave("normed", normed, out_normed)

    def project_group(group):
        at = group * D
        here = slice(group * WIDE, (group + 1) * WIDE)
        shift = jnp.concatenate([vec[4:5, here], jnp.zeros((1, WIDE), f32), vec[5:6, here]], 1)

        def half(part, carry):
            rows = span(part, 512)
            weight = weights[:, :, :, at : at + D].reshape(D, D)
            proj[rows, at : at + D] = (dot_nn(normed[rows, :], weight) + shift).astype(bf16)
            return carry

        lax.fori_loop(0, SEQ // 512, half, 0)

    def attend(group, *calls):
        here = slice(group * WIDE, (group + 1) * WIDE)
        each = SEQ // QUERIES // 4

        def tile(index, carry):
            for inner in range(4):
                rows, value = attend_group(4 * index + inner, group, proj, masks, mixed)
                mixed[rows, here] = value

            @pl.when(index == each // 2 - 1)
            def _():
                for call in calls:
                    call()

            return carry

        lax.fori_loop(0, each, tile, 0)

    def middle_rows():
        leave("both", weights.at[:, :, :, 0 : 4 * D], out_both)
        leave("mixed", mixed, out_mixed)
        leave("proj", proj, out_proj)

        def part(index, carry):
            middle_part(index, tokens, mixed, weights.at[:, :, :, 3 * D : 4 * D], vec, middle, normed_two)
            return carry

        lax.fori_loop(0, SEQ // 512, part, 0)

    hidden, grad_pre, low_final = proj.at[:, 0:D], proj.at[:, D : 2 * D], proj.at[:, 2 * D :]

    def prepare():
        normed_t[...] = normed_two[...].T
        final[...] = middle[...] + vec[7:8, :]
        grad_normed[...] = jnp.zeros_like(grad_normed)
        grad_small[...] = jnp.zeros_like(grad_small)
        lay_out(tiles, 8, bias.shape[1], all_bias)
        for name in ("normed", "both", "mixed", "proj"):
            copies[name].wait()
        u0.drain()
        low_final[...] = grad_middle[...].astype(bf16)
        grad_small[7:8, :] = jnp.sum(low_final[...].astype(f32), 0, keepdims=True)

    up_sum = ReduceStart(place, weights.at[:, :, :, 0 : 2 * D], *up_scratch, near_up, own_up, sum_send.at[0], sum_recv.at[0])
    down_sum = ReducePlanesStart(
        place, weights.at[:, :, :, 2 * D : 4 * D], *down_scratch, near_down, own_down, sum_send.at[1], sum_recv.at[1]
    )

    def chunk_copies(chunk):
        which = chunk - 2
        return (
            pltpu.make_async_copy(
                weights.at[:, :, :, span(2 * chunk, D)], out_up.at[:, :, :, span(which, D)], out_sems.at[10 + which]
            ),
            pltpu.make_async_copy(
                weights.at[:, :, :, span(2 * chunk + 1, D)], out_down.at[:, :, :, span(which, D)], out_sems.at[12 + which]
            ),
        )

    def feed(chunk, carry):
        later = chunk // 2

        def when(value, *calls):
            @pl.when(chunk == value)
            def _():
                for call in calls:
                    call()

        def up_weight():
            return columns(weights, 4 + chunk, D)

        def down_weight():
            return all_down[chunk].reshape(D, D)

        total = jnp.zeros((1, D), f32)
        for block in range(SEQ // 512):
            total = total + feed_rows(
                pl.ds(block * 512, 512), span(chunk, D), normed_two, up_weight, down_weight, all_bias,
                low_final, hidden, grad_pre, final, grad_normed,
            )
        grad_small[pl.ds(8 + chunk, 1), :] = total
        when(0, u1.from_near)
        when(1, u1.from_far, functools.partial(down.from_far, 1))
        when(2, down_sum.to_far, up_sum.to_far)
        when(3, down_sum.pass_sum)
        weights[:, :, :, span(chunk + 2 + later * (chunk - 1), D)] = dot_tn(hidden[...], low_final[...]).astype(bf16).reshape(cut)
        when(1, down_sum.swap, u1.finish)
        when(3, up_sum.pass_sum)
        weights[:, :, :, span(chunk + later * chunk, D)] = dot_nn(normed_t[...], grad_pre[...]).astype(bf16).reshape(cut)
        when(0, functools.partial(down.from_near, 1), old_spread.finish)
        when(1, functools.partial(down.finish, 1), up_sum.swap, u1.drain)

        @pl.when(chunk >= 2)
        def _():
            for copy in chunk_copies(chunk):
                copy.start()

        return carry

    def last_copies(part):
        rows = span(part, 256)
        return (
            pltpu.make_async_copy(hidden.at[rows, :], out_tokens.at[rows, :], out_sems.at[14 + part]),
            pltpu.make_async_copy(grad_middle.at[rows, :], out_middle.at[rows, :], out_sems.at[18 + part]),
        )

    def last():
        def back(part, carry):
            gain, shift = carry
            rows = span(part, 256)
            unit, scale = normalise(middle[rows, :])
            grad = grad_normed[rows, :]
            grad_middle[rows, :] = grad_middle[rows, :] + normalise_back(grad, vec[2:3, :], unit, scale)
            hidden[rows, :] = final[rows, :].astype(bf16)
            for copy in last_copies(part):
                copy.start()
            return gain + jnp.sum(grad * unit, 0, keepdims=True), shift + jnp.sum(grad, 0, keepdims=True)

        zero = jnp.zeros((1, D), f32)
        gain, shift = lax.fori_loop(0, SEQ // 256, back, (zero, zero))
        grad_small[2:3, :] = gain
        grad_small[3:4, :] = shift
        lay_out(olds, 8, bias.shape[1], all_bias)
        moments[...] = jnp.ones_like(moments)
        lay_out(olds, 0, vectors.shape[1], moments.at[0:8, :])
        for index in range(FF // D):
            moments[8 + index : 9 + index, :] = all_bias[0:1, index * D : index * D + D]
        for index in range(ends.shape[1]):
            pooled[0, index : index + 1, :] = final[pl.ds(ends[0, index], 1), :]
        for user in (down, old_spread, up_sum, down_sum):
            user.drain()
        copies["masks"].wait()
        for part in range(4):
            for copy in last_copies(part):
                copy.wait()
        for chunk in (2, 3):
            for copy in chunk_copies(chunk):
                copy.wait()

    begin()
    spread.first()
    lay_qkv()
    g0.swap()
    g1.swap()
    g2.swap()
    lay_rest()
    u0.swap()
    down.swap()
    u1.swap()
    cotangent()
    spread.second()
    g0.own()
    g1.own()
    u0.own()
    spread.third()
    spread.fourth()
    g0.along_z()
    spread.finish()
    norm_tokens()
    g1.along_z()
    g0.from_near()
    g1.from_near()
    g2.own()
    u0.along_z()
    g0.from_far()
    down.own()
    g1.from_far()
    spread.drain()
    g0.finish()
    project_group(0)
    g1.finish()
    old_spread.first()
    attend(0, g2.along_z, old_spread.second)
    project_group(1)
    attend(1)
    g2.from_near()
    u0.from_near()
    g2.from_far()
    down.along_z(0)
    u1.own()
    g2.finish()
    project_group(2)
    attend(2)
    u0.from_far()
    old_spread.third()
    down.from_near(0)
    g0.drain()
    g1.drain()
    g2.drain()
    u0.finish()
    middle_rows()
    u1.along_z()
    down.along_z(1)
    down.from_far(0)
    old_spread.fourth()
    prepare()
    down.finish(0)
    lax.fori_loop(0, FF // D, feed, 0)
    last()


def front_call(
    mesh_shape, tokens, ends, cot_out, cot_pooled, w_qkv, w_out, w_up, w_down, vectors, bias, moment_vec, moment_bias
):
    shape = jax.ShapeDtypeStruct
    line = mesh_shape["dp"] // 2
    rows, tall = w_up.shape[0], w_down.shape[0]
    low, full = pltpu.VMEM((SEQ, D), bf16), pltpu.VMEM((SEQ, D), f32)
    dma = pltpu.SemaphoreType.DMA
    return pl.pallas_call(
        functools.partial(front_kernel, mesh_shape),
        out_shape=(
            shape((line, 2, 4 * rows, 4 * D), bf16),
            shape((SEQ, D), bf16),
            shape((SEQ, 3 * D), bf16),
            shape((SEQ, D), bf16),
            shape((SEQ, D), bf16),
            shape((SEQ, D), f32),
            shape((line, 2, 4 * rows, 2 * D), bf16),
            shape((4, 2, tall, 2 * D), bf16),
            shape((SEQ // QUERIES, WINDOW, GROUP * QUERIES), f32),
            shape((8, D), f32),
            shape((16, D), f32),
            shape((1, ends.shape[1], D), f32),
            shape((16, D), f32),
            shape((line, 2 * rows, D), bf16),
            shape((line, 2 * rows, D), f32),
            shape((2, tall, D), bf16),
            shape((2, tall, D), f32),
        ),
        in_specs=vmem(1) + [SMEM] + vmem(10),
        out_specs=tuple([pl.BlockSpec(memory_space=pl.ANY)] * 9 + vmem(8)),
        scratch_shapes=[
            pltpu.VMEM((rows, 8 * D), f32),
            pltpu.VMEM((2 * rows, 4 * D), f32),
            pltpu.VMEM((2 * tall, D // 2), f32),
            pltpu.VMEM((line, 2, 4 * rows, 8 * D), bf16),
            pltpu.VMEM((line, 2, 4 * tall, D), bf16),
            pltpu.VMEM((line, 2, 2, 2, 16, 128), bf16),
            pltpu.VMEM((line, 2, 2, 2, 16, 128), f32),
            pltpu.VMEM((1, FF), f32),
            low,
            pltpu.VMEM((SEQ, 3 * D), bf16),
            low,
            full,
            low,
            full,
            full,
            full,
            pltpu.VMEM((D, SEQ), bf16),
            pltpu.VMEM((2, SEQ // QUERIES, GROUP * QUERIES), jnp.int32),
            pltpu.VMEM((SEQ // QUERIES, WINDOW, GROUP * QUERIES), f32),
            pltpu.VMEM((96, D), bf16),
            pltpu.VMEM((line, 2, 4 * rows, D), bf16),
            pltpu.VMEM((2, line, 2 * rows, D), bf16),
            pltpu.VMEM((2, line, 2 * rows, D), bf16),
            pltpu.VMEM((4, 2, tall, D), bf16),
            pltpu.VMEM((2, 2, tall, D), bf16),
            pltpu.VMEM((2, 2, tall, D), bf16),
            dma((6, 3 * line)),
            dma((6, 3 * line)),
            dma((2, 3)),
            dma((2, 3)),
            dma((line + 3,)),
            dma((line + 3,)),
            dma((line + 3,)),
            dma((line + 3,)),
            dma((22,)),
        ],
        compiler_params=pltpu.CompilerParams(
            vmem_limit_bytes=FRONT_LIMIT, collective_id=0, has_side_effects=True
        ),
        name="front",
    )(tokens, ends, cot_out, cot_pooled, w_qkv, w_out, w_up, w_down, vectors, bias, moment_vec, moment_bias)


FRONT_LIMIT = 62 * 1024 * 1024


def attend_group_back(tile, group, proj, masks, grad_mixed):
    start = window_start(tile)
    rows, window, at = span(tile, QUERIES), pl.ds(start, WINDOW), group * D
    mask = masks[tile]
    queries = split_heads(scaled(proj[rows, at : at + WIDE]))
    grads = split_heads(grad_mixed[rows, group * WIDE : (group + 1) * WIDE])
    keys = proj[window, at + WIDE : at + 2 * WIDE]
    values = proj[window, at + 2 * WIDE : at + D]
    probs = probabilities(keys, queries, mask)
    grad_probs = dot_nt(values, grads)
    along = jnp.sum(probs * grad_probs, 0, keepdims=True)
    grad_scores = (probs * (grad_probs - along)).astype(bf16)
    both = join_heads(dot_tn(grad_scores, keys)) * HEAD_DIM ** (-0.5)
    return rows, window, both.astype(bf16), dot_nn(grad_scores, queries), dot_nn(probs.astype(bf16), grads)


def rear_kernel(mesh_shape, *refs):
    refs = list(refs)

    def take(count):
        taken = refs[:count]
        del refs[:count]
        return taken

    from_tokens, ends, from_both, vec, moments, small = take(6)
    from_proj, from_normed, from_mixed, from_middle, from_up, from_down, from_masks = take(7)
    near_up, own_up, near_down, own_down = take(4)
    weights, (vectors, bias), rows = take(4), take(2), take(4)
    out_tokens, grads, (grad_vec, grad_bias, stats) = take(1)[0], take(4), take(3)
    proj, spare, turned, low_middle, grad_mixed, grad_keys, grad_values, grad_middle, masks, w_both, tokens = take(11)
    term_out, term_groups, part_out, part_groups = take(4)
    up_rest, down_rest = take(4), take(4)
    up_mine, up_scratch, down_mine, down_scratch = take(1)[0], take(8), take(1)[0], take(8)
    scratch = take(8)
    early, late, send, recv, sems, load_sems = take(5), take(5), *take(4)
    place = Place(mesh_shape)
    line = place.line
    cut = (line, 2, D // (2 * line), D)
    def load(index, source, target):
        size = target.shape[0] // 4
        return [
            pltpu.make_async_copy(source.at[pl.ds(part * size, size)], target.at[pl.ds(part * size, size)], load_sems.at[index, part])
            for part in range(4)
        ]

    def wait_for(index):
        for copy in loads[index]:
            copy.wait()

    out_part, qkv_part = slice(3 * D, 4 * D), slice(0, 3 * D)
    loads = [
        load(0, from_middle, grad_middle),
        load(1, from_both.at[:, :, :, out_part], w_both.at[:, :, :, out_part]),
        load(2, from_mixed, spare),
        load(3, from_proj, proj),
        load(4, from_masks, masks),
        load(5, from_both.at[:, :, :, qkv_part], w_both.at[:, :, :, qkv_part]),
        load(6, from_tokens, tokens),
    ]
    normed_copy = pltpu.make_async_copy(from_normed, spare, sems.at[0])
    token_copies = [
        pltpu.make_async_copy(grad_middle.at[at : at + 512, :], out_tokens.at[at : at + 512, :], sems.at[1 + at // 512])
        for at in range(0, SEQ, 512)
    ]

    half_up = grads[2].at[:, 0 : 2 * D], grads[2].at[:, 2 * D :]
    u0 = ReduceRest(place, near_up, own_up, *up_rest, half_up[0], send.at[0], recv.at[0])
    d0 = ReducePlanesRest(place, 0, near_down, own_down, *down_rest, grads[3], send.at[1], recv.at[1])
    u1 = Reduce(place, from_up, *[ref.at[0] for ref in up_scratch], half_up[1], send.at[2], recv.at[2], up_mine)
    d1 = ReducePlanes(
        place, 2, from_down, *[ref.at[0] for ref in down_scratch], grads[3], send.at[3], recv.at[3], down_mine
    )

    def attention_of(index):
        term, part = (term_groups.at[index], part_groups.at[index]) if index < 3 else (term_out, part_out)
        return Reduce(place, term, *[ref.at[index] for ref in scratch], part, send.at[4 + index], recv.at[4 + index])

    g0, g1, g2, out = (attention_of(index) for index in range(4))
    early_sum, late_sum = AllSum(place, *early), AllSum(place, *late)
    first, second = early[0], late[0]
    local = LocalTerms(weights, rows)

    def begin():
        for copies in loads:
            for copy in copies:
                copy.start()
        greet(place)

    def prepare():
        first[...] = jnp.zeros_like(first)
        first[0:16, :] = small[...]
        second[...] = jnp.zeros_like(second)
        wait_for(0)
        wait_for(1)

    def out_back():
        w_out = w_both.at[:, :, :, 3 * D :]

        def out_part(part, total):
            return out_back_part(part, grad_middle, w_out, low_middle, grad_mixed, total)

        first[6:7, :] = lax.fori_loop(0, SEQ // 512, out_part, jnp.zeros((1, D), f32))

    def out_grad():
        wait_for(2)
        turned[...] = spare[...].T
        normed_copy.start()

        def third(part, carry):
            term = dot_nn(turned[...], low_middle[:, span(part, WIDE)]).astype(bf16)
            term_out[:, :, :, span(part, WIDE)] = term.reshape(cut[:3] + (WIDE,))
            return carry

        lax.fori_loop(0, 3, third, 0)
        normed_copy.wait()
        turned[...] = spare[...].T
        wait_for(3)
        wait_for(4)

    def tiles(group, *calls):
        at = group * D
        each = SEQ // QUERIES // 4
        grad_keys[...] = jnp.zeros_like(grad_keys)
        grad_values[...] = jnp.zeros_like(grad_values)

        def tile(index, carry):
            done = [attend_group_back(4 * index + inner, group, proj, masks, grad_mixed) for inner in range(4)]
            for where, window, query, key, value in done:
                proj[where, at : at + WIDE] = query
                grad_keys[window, :] += key
                grad_values[window, :] += value

            @pl.when(index == each // 2 - 1)
            def _():
                for call in calls:
                    call()

            return carry

        lax.fori_loop(0, each, tile, 0)

    def group_grad(group):
        at = group * D
        here = slice(group * WIDE, (group + 1) * WIDE)
        proj[:, at + WIDE : at + 2 * WIDE] = grad_keys[...].astype(bf16)
        proj[:, at + 2 * WIDE : at + D] = grad_values[...].astype(bf16)

        def third(part, carry):
            term = dot_nn(turned[...], proj[:, span(3 * group + part, WIDE)]).astype(bf16)
            term_groups[group, :, :, :, span(part, WIDE)] = term.reshape(cut[:3] + (WIDE,))
            return carry

        lax.fori_loop(0, 3, third, 0)
        first[4:5, here] = jnp.sum(proj[:, at : at + WIDE].astype(f32), 0, keepdims=True)
        first[5:6, here] = jnp.sum(proj[:, at + 2 * WIDE : at + D].astype(f32), 0, keepdims=True)

    def tokens_part(part):
        if part == 0:
            wait_for(5)
            wait_for(6)

        def quarter(index, carry):
            where = span(2 * part + index, 256)
            grad = dot_nt(proj[where, :], w_both[:, :, :, 0 : 3 * D].reshape(D, 3 * D))
            unit, scale = normalise(tokens[where, :].astype(f32))
            grad_middle[where, :] = grad_middle[where, :] + normalise_back(grad, vec[0:1, :], unit, scale)
            second[0:1, :] = second[0:1, :] + jnp.sum(grad * unit, 0, keepdims=True)
            second[1:2, :] = second[1:2, :] + jnp.sum(grad, 0, keepdims=True)
            return carry

        lax.fori_loop(0, 2, quarter, 0)
        token_copies[part].start()

    def feed_terms():
        local.matrix(2, grads[2], first, 16)
        local.matrix(3, grads[3], first, 24)
        local.rest(vectors, bias)
        first[26:27, :] = local.sums

    def out_terms():
        grads[1][...] = part_out[...]
        local.matrix(1, grads[1], first, 27)

    def qkv_terms():
        for index in range(3):
            for piece in range(3):
                at = piece * D + index * WIDE
                grads[0][:, at : at + WIDE] = part_groups[index, :, piece * WIDE : (piece + 1) * WIDE]
        local.matrix(0, grads[0], second, 2)

    def last():
        first[0:2, :] = second[0:2, :]
        grad_vec[...] = own_vectors(place, first, vectors.shape[1])
        grad_bias[...] = own_bias(place, first, bias.shape[1])
        grad = first[0:16, :]
        update = grad * lax.rsqrt(moment_of(grad, moments[...]))
        lane = lax.broadcasted_iota(jnp.int32, (1, D), 1)
        stats[...] = jnp.zeros_like(stats)
        stats[0:3, :] = second[2:5, :]
        stats[3:4, :] = first[27:28, :]
        stats[4:8, :] = first[16:20, :]
        stats[8:9, :] = first[24:25, :]
        stats[9:12, :] = second[5:8, :]
        stats[12:13, :] = first[28:29, :]
        stats[13:17, :] = first[20:24, :]
        stats[17:18, :] = first[25:26, :]
        stats[18:19, :] = jnp.where(lane == 17, total(update * update), first[26:27, :])
        for copy in token_copies:
            copy.wait()

    begin()
    u1.swap()
    u0.to_near()
    d0.to_near()
    prepare()
    out_back()
    u1.to_far()
    out_grad()
    out.swap()
    tiles(0, u0.to_line, out.to_far, d0.to_line, d1.swap)
    u1.to_near()
    out.to_near()
    d1.to_far()
    group_grad(0)
    tiles(1, u0.to_owner)
    u0.finish()
    out.to_line()
    u1.to_line()
    g0.swap()
    group_grad(1)
    g1.swap()
    d1.to_near()
    tiles(2, g0.to_far, g1.to_far, d1.to_line, d1.to_owner, d1.finish)
    out.to_owner()
    d0.to_owner()
    u1.to_owner()
    d0.finish()
    group_grad(2)
    g0.to_near()
    out.finish()
    g1.to_near()
    g2.swap()
    out_terms()
    u1.finish()
    feed_terms()
    g2.to_far()
    early_sum.start(0)
    g0.to_line()
    g1.to_line()
    tokens_part(0)
    g2.to_near()
    early_sum.next(0)
    tokens_part(1)
    g0.to_owner()
    g1.to_owner()
    early_sum.next(1)
    g2.to_line()
    g0.finish()
    g1.finish()
    early_sum.next(2)
    g2.to_owner()
    g2.finish()
    qkv_terms()
    late_sum.start(0)
    u0.drain()
    d0.drain()
    u1.drain()
    late_sum.next(0)
    d1.drain()
    out.drain()
    late_sum.next(1)
    g0.drain()
    g1.drain()
    late_sum.next(2)
    g2.drain()
    late_sum.end_line()
    early_sum.end_line()
    last()


class LocalTerms:
    def __init__(self, weights, rows):
        self.weights, self.rows = weights, rows
        self.lane = lax.broadcasted_iota(jnp.int32, (1, D), 1)
        self.sums = jnp.zeros((1, D), f32)

    def matrix(self, index, source, value, at):
        grad = source[...]
        row = row_statistic(grad, self.rows[index][...])
        square = grad * grad
        line = jnp.sum(square + square_eps, 0, keepdims=True)
        weighed = jnp.sum(square * (1.0 / row), 0, keepdims=True)
        count = grad.shape[1] // D
        for part in range(count):
            value[at + part : at + part + 1, :] = line[:, part * D : part * D + D]
            value[at + count + part : at + count + part + 1, :] = weighed[:, part * D : part * D + D]

    def rest(self, vectors, bias):
        for index in range(4):
            weight = self.weights[index][...]
            old = jnp.sum(self.rows[index][...], 1, keepdims=True)
            self.sums = jnp.where(self.lane == index, old, self.sums)
            self.sums = jnp.where(self.lane == 4 + index, total(weight * weight), self.sums)
        squares = jnp.sum(vectors[...] * vectors[...], 1, keepdims=True)
        for index in range(8):
            self.sums = jnp.where(self.lane == 8 + index, squares[index : index + 1, :], self.sums)
        self.sums = jnp.where(self.lane == 16, total(bias[...] * bias[...]), self.sums)


def rear_call(
    mesh_shape, tokens, ends, w_both, vec, moments, small, proj, normed, mixed, middle, terms, sums, weights, vectors, bias, rows
):
    shape = jax.ShapeDtypeStruct
    line = mesh_shape["dp"] // 2
    low = pltpu.VMEM((SEQ, D), bf16)
    tall, deep = weights[2].shape[0], weights[3].shape[0]
    cut = (line, 2, 4 * tall)
    far = pl.BlockSpec(memory_space=pl.ANY)
    return pl.pallas_call(
        functools.partial(rear_kernel, mesh_shape),
        out_shape=(shape((SEQ, D), f32),)
        + tuple(shape(w.shape, f32) for w in weights)
        + (shape(vectors.shape, f32), shape(bias.shape, f32), shape((24, D), f32)),
        in_specs=[far, SMEM, far] + vmem(3) + [far] * 7 + vmem(14),
        out_specs=tuple([pl.BlockSpec(memory_space=pl.ANY)] + vmem(7)),
        scratch_shapes=[
            pltpu.VMEM((SEQ, 3 * D), bf16),
            low,
            pltpu.VMEM((D, SEQ), bf16),
            low,
            low,
            pltpu.VMEM((SEQ, WIDE), f32),
            pltpu.VMEM((SEQ, WIDE), f32),
            pltpu.VMEM((SEQ, D), f32),
            pltpu.VMEM((SEQ // QUERIES, WINDOW, GROUP * QUERIES), f32),
            pltpu.VMEM(w_both.shape, bf16),
            low,
            pltpu.VMEM(cut + (D,), bf16),
            pltpu.VMEM((3,) + cut + (D,), bf16),
            pltpu.VMEM((tall, D), f32),
            pltpu.VMEM((3, tall, D), f32),
            pltpu.VMEM((line, 2 * tall, D), bf16),
            pltpu.VMEM((line - 1, 2 * tall, D), bf16),
            pltpu.VMEM((line - 1, 2 * tall, D), bf16),
            pltpu.VMEM((2 * tall, D), f32),
            pltpu.VMEM((2, deep, D), bf16),
            pltpu.VMEM((2, deep, D), bf16),
            pltpu.VMEM((line - 1, 2, deep, D), bf16),
            pltpu.VMEM((2, deep, D), f32),
            pltpu.VMEM(cut + (D,), bf16),
        ]
        + reduce_scratch(line, 2 * tall, D, 1)
        + [pltpu.VMEM((4, 2, deep, D), bf16)]
        + plane_scratch(line, deep, D, 1)
        + reduce_scratch(line, 2 * tall, D // 2, 4)
        + sum_scratch(line, 32)
        + sum_scratch(line, 8)
        + [pltpu.SemaphoreType.DMA((8, 5 + line))] * 2
        + [pltpu.SemaphoreType.DMA((3,)), pltpu.SemaphoreType.DMA((7, 4))],
        compiler_params=pltpu.CompilerParams(
            vmem_limit_bytes=FRONT_LIMIT, collective_id=1, has_side_effects=True
        ),
        name="rear",
    )(tokens, ends, w_both, vec, moments, small, proj, normed, mixed, middle, *terms, *sums, *weights, vectors, bias, *rows)


def plain_device(
    tokens,
    ends,
    cot_out,
    cot_pooled,
    w_qkv,
    w_out,
    w_up,
    w_down,
    vectors,
    bias_up,
    row_qkv,
    col_qkv,
    row_out,
    col_out,
    row_up,
    col_up,
    row_down,
    col_down,
    moment_vectors,
    moment_bias_up,
):
    low_qkv = w_qkv.astype(jnp.bfloat16)
    low_out = w_out.astype(jnp.bfloat16)
    low_up = w_up.astype(jnp.bfloat16)
    low_down = w_down.astype(jnp.bfloat16)
    low_vec = vectors.astype(jnp.bfloat16)
    low_upbias = bias_up.astype(jnp.bfloat16)
    gathered = (
        lax.all_gather(low_qkv, ("dp", "fsdp"), axis=0, tiled=True),
        lax.all_gather(low_out, ("dp", "fsdp"), axis=0, tiled=True),
        lax.all_gather(low_up, ("dp", "fsdp"), axis=0, tiled=True),
        lax.all_gather(low_down, ("dp", "fsdp"), axis=0, tiled=True),
        lax.all_gather(low_vec, ("dp", "fsdp"), axis=0, tiled=True),
        lax.all_gather(low_upbias, ("dp", "fsdp"), axis=0, tiled=True),
    )
    qkv_full, out_full, up_full, down_full = (gathered[0], gathered[1], gathered[2], gathered[3])
    vec_full = gathered[4].astype(jnp.float32)
    upbias_full = gathered[5].astype(jnp.float32)
    vec = vec_full.T
    bias = upbias_full.reshape(1, FF)
    normed, proj, mixed, middle, normed_two = forward_call(tokens, ends, qkv_full, out_full, vec)
    out_tokens, pooled, grad_middle, grad_w_up, grad_w_down, small = feed_call(
        normed_two, middle, up_full, down_full, vec, bias, cot_out, cot_pooled, ends
    )
    grad_tokens, grad_w_qkv, grad_w_out, small = backward_call(
        tokens, ends, qkv_full, out_full, vec, normed, proj, mixed, grad_middle, small
    )
    grad_vectors = small[:8].T
    grad_bias_up = small[8:12].reshape(FF)
    summed_up, summed_down, summed_upbias = (
        lax.psum_scatter(grad_w_up.astype(f32), ("dp", "fsdp"), scatter_dimension=0, tiled=True),
        lax.psum_scatter(grad_w_down.astype(f32), ("dp", "fsdp"), scatter_dimension=0, tiled=True),
        lax.psum_scatter(grad_bias_up, ("dp", "fsdp"), scatter_dimension=0, tiled=True),
    )
    summed_qkv, summed_out, summed_vec = (
        lax.psum_scatter(grad_w_qkv.astype(f32), ("dp", "fsdp"), scatter_dimension=0, tiled=True),
        lax.psum_scatter(grad_w_out.astype(f32), ("dp", "fsdp"), scatter_dimension=0, tiled=True),
        lax.psum_scatter(grad_vectors, ("dp", "fsdp"), scatter_dimension=0, tiled=True),
    )
    matrices = (summed_qkv, summed_out, summed_up, summed_down)
    old_rows = (row_qkv, row_out, row_up, row_down)
    old_cols = (col_qkv, col_out, col_up, col_down)
    masters = (w_qkv, w_out, w_up, w_down)
    row_sizes = (D, D, D, FF)
    tensor_sizes = (3 * D * D, D * D, D * FF, FF * D)
    squares = [gradient * gradient + square_eps for gradient in matrices]
    rows_new = [
        decay * old + (1.0 - decay) * jnp.mean(square, 1) for old, square in zip(old_rows, squares)
    ]
    col_parts = [jnp.sum(square, 0) for square in squares]
    local_totals = jnp.concatenate(
        [
            jnp.stack([jnp.sum(renewed) for renewed in rows_new]),
            jnp.stack([jnp.sum(master * master) for master in masters]),
            jnp.sum(vectors * vectors, 0),
            jnp.sum(bias_up * bias_up)[None],
        ]
    )
    col_sum_qkv, col_sum_out, col_sum_up, col_sum_down, global_totals = lax.psum(
        (col_parts[0], col_parts[1], col_parts[2], col_parts[3], local_totals), ("dp", "fsdp")
    )
    col_sums = (col_sum_qkv, col_sum_out, col_sum_up, col_sum_down)
    cols_new = [
        decay * old + (1.0 - decay) * (summed / count)
        for old, summed, count in zip(old_cols, col_sums, row_sizes)
    ]
    updates = []
    for index_mat in range(4):
        row_mean = global_totals[index_mat] / row_sizes[index_mat]
        renewed_row = rows_new[index_mat]
        renewed_col = cols_new[index_mat]
        updates.append(
            matrices[index_mat] * lax.rsqrt(renewed_row[:, None] * renewed_col[None, :] / row_mean)
        )
    moment_vec = decay * moment_vectors + (1.0 - decay) * (summed_vec * summed_vec + square_eps)
    update_vec = summed_vec * lax.rsqrt(moment_vec)
    moment_upb = decay * moment_bias_up + (1.0 - decay) * (
        summed_upbias * summed_upbias + square_eps
    )
    update_upb = summed_upbias * lax.rsqrt(moment_upb)
    local_norm = jnp.sum(update_vec * update_vec) + jnp.sum(update_upb * update_upb)
    for update in updates:
        local_norm = local_norm + jnp.sum(update * update)
    norm_total = lax.psum(local_norm, ("dp", "fsdp"))
    param_count = 4 * D * D + 2 * D * FF + 8 * D + FF
    clip = jnp.maximum(1.0, jnp.sqrt(norm_total / param_count) / clip_limit)
    new_weights = []
    for index_mat in range(4):
        scale = jnp.maximum(
            scale_floor, jnp.sqrt(global_totals[4 + index_mat] / tensor_sizes[index_mat])
        )
        new_weights.append(masters[index_mat] - step_rate * scale * updates[index_mat] / clip)
    vec_scale = jnp.maximum(scale_floor, jnp.sqrt(global_totals[8:16] / D))[None, :]
    new_vec = vectors - step_rate * vec_scale * update_vec / clip
    upb_scale = jnp.maximum(scale_floor, jnp.sqrt(global_totals[16] / FF))
    new_upb = bias_up - step_rate * upb_scale * update_upb / clip
    return (
        out_tokens,
        pooled,
        grad_tokens,
        summed_qkv,
        rows_new[0],
        cols_new[0],
        new_weights[0],
        summed_out,
        rows_new[1],
        cols_new[1],
        new_weights[1],
        summed_up,
        rows_new[2],
        cols_new[2],
        new_weights[2],
        summed_down,
        rows_new[3],
        cols_new[3],
        new_weights[3],
        summed_vec,
        moment_vec,
        new_vec,
        summed_upbias,
        moment_upb,
        new_upb,
        clip,
    )


def kernels_fit(mesh_shape):
    rows = D // (mesh_shape["dp"] * mesh_shape["fsdp"])
    return mesh_shape["fsdp"] == 4 and mesh_shape["dp"] == 8 and rows % 8 == 0


def per_device(
    mesh_shape,
    tokens,
    ends,
    cot_out,
    cot_pooled,
    w_qkv,
    w_out,
    w_up,
    w_down,
    vectors,
    bias_up,
    row_qkv,
    col_qkv,
    row_out,
    col_out,
    row_up,
    col_up,
    row_down,
    col_down,
    moment_vectors,
    moment_bias_up,
):
    def whole(array):
        return array.reshape(-1, array.shape[-1])

    def row(array):
        return array.reshape(1, -1)

    bias_row = row(bias_up)
    moments = (moment_vectors.T, row(moment_bias_up))
    both, normed, proj, mixed, out_tokens, grad_middle, *terms, vec, all_moments, pooled, small, a, b, e, f = front_call(
        mesh_shape, tokens, ends, cot_out, cot_pooled, w_qkv, w_out, w_up, w_down, vectors.T, bias_row, *moments
    )
    weights = (w_qkv, w_out, w_up, w_down)
    rows = [row(value) for value in (row_qkv, row_out, row_up, row_down)]
    cols = [col_qkv, col_out, col_up, col_down]
    grad_tokens, *summed = rear_call(
        mesh_shape, tokens, ends, both, vec, all_moments, small, proj, normed, mixed, grad_middle,
        terms, (a, b, e, f), weights, vectors.T, bias_row, rows
    )
    large = (out_tokens, pooled, grad_tokens)
    done = finish_call(large, summed, weights, vectors.T, bias_row, rows, cols, *moments)
    results, done = list(done[:3]), done[3:]
    for index in range(4):
        results += [done[index], done[4 + index].reshape(-1), done[8 + index], done[12 + index]]
    results += [value.T for value in done[16:19]] + [value.reshape(-1) for value in done[19:22]]
    return tuple(results + [done[22].reshape(())])


def solution(mesh):
    in_specs = (
        P(("dp", "fsdp"), None),
        P(("dp", "fsdp"), None),
        P(("dp", "fsdp"), None),
        P(("dp", "fsdp"), None, None),
        P(("dp", "fsdp"), None),
        P(("dp", "fsdp"), None),
        P(("dp", "fsdp"), None),
        P(("dp", "fsdp"), None),
        P(("dp", "fsdp"), None),
        P(("dp", "fsdp")),
        P(("dp", "fsdp")),
        P(),
        P(("dp", "fsdp")),
        P(),
        P(("dp", "fsdp")),
        P(),
        P(("dp", "fsdp")),
        P(),
        P(("dp", "fsdp"), None),
        P(("dp", "fsdp")),
    )
    out_specs = (
        P(("dp", "fsdp"), None),
        P(("dp", "fsdp"), None, None),
        P(("dp", "fsdp"), None),
        P(("dp", "fsdp"), None),
        P(("dp", "fsdp")),
        P(),
        P(("dp", "fsdp"), None),
        P(("dp", "fsdp"), None),
        P(("dp", "fsdp")),
        P(),
        P(("dp", "fsdp"), None),
        P(("dp", "fsdp"), None),
        P(("dp", "fsdp")),
        P(),
        P(("dp", "fsdp"), None),
        P(("dp", "fsdp"), None),
        P(("dp", "fsdp")),
        P(),
        P(("dp", "fsdp"), None),
        P(("dp", "fsdp"), None),
        P(("dp", "fsdp"), None),
        P(("dp", "fsdp"), None),
        P(("dp", "fsdp")),
        P(("dp", "fsdp")),
        P(("dp", "fsdp")),
        P(),
    )
    fits = kernels_fit(mesh.shape)
    step = functools.partial(per_device, dict(mesh.shape)) if fits else plain_device
    return jax.shard_map(
        step, mesh=mesh, in_specs=in_specs, out_specs=out_specs, check_vma=False
    )
```

```python
import functools

import jax
import jax.numpy as jnp
from jax import lax
from jax.experimental import pallas as pl
from jax.experimental.pallas import tpu as pltpu
from jax.sharding import PartitionSpec as P

D = 768
HEADS = 12
HEAD_DIM = 64
FF = 3072
SEQ = 1024
STEP = 10
REACH = 64
QUERIES = 64
WINDOW = 192
GROUP = 4
WIDE = GROUP * HEAD_DIM

norm_eps = 1e-06
square_eps = 1e-30
clip_limit = 1.0
step_rate = 0.5
scale_floor = 0.001
decay = 1.0 - STEP ** (-0.8)

f32 = jnp.float32
bf16 = jnp.bfloat16
MESH = pl.DeviceIdType.MESH
VMEM_LIMIT = 60 * 1024 * 1024


def dot_nn(left, right):
    return jnp.dot(left, right, preferred_element_type=f32)


def dot_tn(left, right):
    return lax.dot_general(left, right, (((0,), (0,)), ((), ())), preferred_element_type=f32)


def dot_nt(left, right):
    return lax.dot_general(left, right, (((1,), (1,)), ((), ())), preferred_element_type=f32)


def span(index, size):
    return pl.ds(pl.multiple_of(index * size, size), size)


def columns(ref, index, size):
    cut = ref[(slice(None),) * (len(ref.shape) - 1) + (span(index, size),)]
    return cut.reshape(-1, size)


def normalise(values):
    centre = jnp.mean(values, -1, keepdims=True)
    centred = values - centre
    scale = lax.rsqrt(jnp.mean(centred * centred, -1, keepdims=True) + norm_eps)
    return centred * scale, scale


def normalise_back(grad, gain, unit, scale):
    inner = grad * gain
    along = jnp.mean(inner * unit, -1, keepdims=True)
    return scale * (inner - jnp.mean(inner, -1, keepdims=True) - unit * along)


def caption_bounds(ends, bounds):
    shape = (SEQ // QUERIES, GROUP * QUERIES)
    places = lax.broadcasted_iota(jnp.int32, shape, 0) * QUERIES
    places = places + lax.rem(lax.broadcasted_iota(jnp.int32, shape, 1), QUERIES)
    first = jnp.zeros(shape, jnp.int32)
    last = jnp.full(shape, SEQ - 1, jnp.int32)
    for index in range(ends.shape[1]):
        end = ends[0, index]
        first = jnp.where(places > end, jnp.maximum(first, end + 1), first)
        last = jnp.where(places <= end, jnp.minimum(last, end), last)
    bounds[0] = first
    bounds[1] = last


def tile_mask(bounds, tile, start):
    places = start + lax.broadcasted_iota(jnp.int32, (WINDOW, GROUP * QUERIES), 0)
    row = pl.ds(tile, 1)
    inside = (places >= bounds[0, row, :]) & (places <= bounds[1, row, :])
    return jnp.where(inside, 0.0, -1e30).astype(f32)


def window_start(tile):
    start = jnp.clip(tile * QUERIES - REACH, 0, SEQ - WINDOW)
    return pl.multiple_of(start, REACH)


def head_of(shape):
    return lax.broadcasted_iota(jnp.int32, shape, 1) // HEAD_DIM


def split_heads(rows):
    head, zero = head_of(rows.shape), jnp.zeros_like(rows)
    return jnp.concatenate([jnp.where(head == index, rows, zero) for index in range(GROUP)], 0)


def join_heads(blocks):
    shape = (blocks.shape[0] // GROUP, blocks.shape[1])
    head, result = head_of(shape), blocks[: shape[0]]
    for index in range(1, GROUP):
        result = jnp.where(head == index, blocks[index * shape[0] : (index + 1) * shape[0]], result)
    return result


def probabilities(keys, queries, mask):
    scores = dot_nt(keys, queries) + mask
    expo = jnp.exp(scores - jnp.max(scores, 0, keepdims=True))
    return expo * (1.0 / jnp.sum(expo, 0, keepdims=True))


def scaled(queries):
    return queries * jnp.asarray(HEAD_DIM ** (-0.5), queries.dtype)


def first_norm(tokens, vec, normed):
    def step(part, carry):
        rows = span(part, 256)
        unit, _ = normalise(tokens[rows, :].astype(f32))
        normed[rows, :] = (unit * vec[0:1, :] + vec[1:2, :]).astype(bf16)
        return carry

    lax.fori_loop(0, SEQ // 256, step, 0)


def project(normed, w_qkv, vec, proj):
    def step(part, carry):
        weight = columns(w_qkv, part, D)
        shift = jnp.where(part == 0, vec[4:5, :], jnp.where(part == 2, vec[5:6, :], 0.0))
        for half in range(2):
            rows = pl.ds(half * 512, 512)
            proj[rows, span(part, D)] = (dot_nn(normed[rows, :], weight) + shift).astype(bf16)
        return carry

    lax.fori_loop(0, 3, step, 0)


def attend_tile(tile, proj, bounds, mixed):
    start = window_start(tile)
    rows, window = span(tile, QUERIES), pl.ds(start, WINDOW)
    mask = tile_mask(bounds, tile, start)
    for at in range(0, D, WIDE):
        queries = split_heads(scaled(proj[rows, at : at + WIDE]))
        keys = proj[window, D + at : D + at + WIDE]
        values = proj[window, 2 * D + at : 2 * D + at + WIDE]
        probs = probabilities(keys, queries, mask).astype(bf16)
        mixed[rows, at : at + WIDE] = join_heads(dot_tn(probs, values)).astype(bf16)


def middle_part(part, tokens, mixed, w_out, vec, middle, normed):
    rows = span(part, 512)
    weight = w_out[...].reshape(D, D)
    value = tokens[rows, :].astype(f32) + (dot_nn(mixed[rows, :], weight) + vec[6:7, :])
    middle[rows, :] = value
    unit, _ = normalise(value)
    normed[rows, :] = (unit * vec[2:3, :] + vec[3:4, :]).astype(bf16)


def forward_kernel(tokens, ends, w_qkv, w_out, vec, normed, proj, mixed, middle, normed_two, bounds):
    first_norm(tokens, vec, normed)
    project(normed, w_qkv, vec, proj)
    caption_bounds(ends, bounds)

    def tile(index, carry):
        attend_tile(2 * index, proj, bounds, mixed)
        attend_tile(2 * index + 1, proj, bounds, mixed)
        return carry

    lax.fori_loop(0, SEQ // QUERIES // 2, tile, 0)

    def part(index, carry):
        middle_part(index, tokens, mixed, w_out, vec, middle, normed_two)
        return carry

    lax.fori_loop(0, SEQ // 512, part, 0)


def vmem(count):
    return [pl.BlockSpec(memory_space=pltpu.VMEM)] * count


SMEM = pl.BlockSpec(memory_space=pltpu.SMEM)


def forward_call(tokens, ends, w_qkv, w_out, vec):
    shape = jax.ShapeDtypeStruct
    return pl.pallas_call(
        forward_kernel,
        out_shape=(
            shape((SEQ, D), bf16),
            shape((SEQ, 3 * D), bf16),
            shape((SEQ, D), bf16),
            shape((SEQ, D), f32),
            shape((SEQ, D), bf16),
        ),
        in_specs=vmem(1) + [SMEM] + vmem(3),
        out_specs=tuple(vmem(5)),
        scratch_shapes=[pltpu.VMEM((2, SEQ // QUERIES, GROUP * QUERIES), jnp.int32)],
        compiler_params=pltpu.CompilerParams(vmem_limit_bytes=VMEM_LIMIT),
        name="forward",
    )(tokens, ends, w_qkv, w_out, vec)


def feed_kernel(
    normed,
    middle,
    w_up,
    w_down,
    vec,
    bias,
    cot_out,
    cot_pooled,
    ends,
    out,
    pooled,
    grad_middle,
    grad_up,
    grad_down,
    grad_small,
    final,
    grad_final,
    low_final,
    grad_normed,
    normed_t,
    hidden,
    grad_pre,
):
    wide, tall = D, 512
    grad_final[...] = cot_out[...].astype(f32)
    for index in range(ends.shape[1]):
        row = pl.ds(ends[0, index], 1)
        grad_final[row, :] = grad_final[row, :] + cot_pooled[0, index : index + 1, :]
    low_final[...] = grad_final[...].astype(bf16)
    grad_small[...] = jnp.zeros_like(grad_small)
    grad_small[7:8, :] = jnp.sum(low_final[...].astype(f32), 0, keepdims=True)
    final[...] = middle[...] + vec[7:8, :]
    grad_normed[...] = jnp.zeros_like(grad_normed)
    normed_t[...] = normed[...].T
    root = 0.7978845608028654
    cube = 0.044715

    def chunk(part, carry):
        place = span(part, wide)
        shift = bias[:, place]

        def rows_step(block, total):
            rows = span(block, tall)
            pre = dot_nn(normed[rows, :], w_up[:, place]) + shift
            square = pre * pre
            bend = jnp.tanh(root * (pre + cube * (square * pre)))
            half = 0.5 * (1.0 + bend)
            slope = half + 0.5 * pre * (1.0 - bend * bend) * (root + (3.0 * root * cube) * square)
            act = (pre * half).astype(bf16)
            hidden[rows, :] = act
            final[rows, :] = final[rows, :] + dot_nn(act, w_down[place, :])
            back = (dot_nt(low_final[rows, :], w_down[place, :]) * slope).astype(bf16)
            grad_pre[rows, :] = back
            grad_normed[rows, :] = grad_normed[rows, :] + dot_nt(back, w_up[:, place])
            return total + jnp.sum(back.astype(f32), 0, keepdims=True)

        total = lax.fori_loop(0, SEQ // tall, rows_step, jnp.zeros((1, wide), f32))
        grad_small[pl.ds(8 + part, 1), :] = total
        grad_down[place, :] = dot_tn(hidden[...], low_final[...]).astype(bf16)
        grad_up[:, place] = dot_nn(normed_t[...], grad_pre[...]).astype(bf16)
        return carry

    lax.fori_loop(0, FF // wide, chunk, 0)
    out[...] = final[...].astype(bf16)
    for index in range(ends.shape[1]):
        pooled[0, index : index + 1, :] = final[pl.ds(ends[0, index], 1), :]

    def back(part, carry):
        gain, shift = carry
        rows = span(part, 256)
        unit, scale = normalise(middle[rows, :])
        grad = grad_normed[rows, :]
        grad_middle[rows, :] = grad_final[rows, :] + normalise_back(grad, vec[2:3, :], unit, scale)
        return gain + jnp.sum(grad * unit, 0, keepdims=True), shift + jnp.sum(grad, 0, keepdims=True)

    zero = jnp.zeros((1, D), f32)
    gain, shift = lax.fori_loop(0, SEQ // 256, back, (zero, zero))
    grad_small[2:3, :] = gain
    grad_small[3:4, :] = shift


def feed_call(normed, middle, w_up, w_down, vec, bias, cot_out, cot_pooled, ends):
    shape = jax.ShapeDtypeStruct
    count = ends.shape[1]
    return pl.pallas_call(
        feed_kernel,
        out_shape=(
            shape((SEQ, D), bf16),
            shape((1, count, D), f32),
            shape((SEQ, D), f32),
            shape((D, FF), bf16),
            shape((FF, D), bf16),
            shape((16, D), f32),
        ),
        in_specs=vmem(8) + [SMEM],
        out_specs=tuple(vmem(6)),
        scratch_shapes=[
            pltpu.VMEM((SEQ, D), f32),
            pltpu.VMEM((SEQ, D), f32),
            pltpu.VMEM((SEQ, D), bf16),
            pltpu.VMEM((SEQ, D), f32),
            pltpu.VMEM((D, SEQ), bf16),
            pltpu.VMEM((SEQ, D), bf16),
            pltpu.VMEM((SEQ, D), bf16),
        ],
        compiler_params=pltpu.CompilerParams(vmem_limit_bytes=VMEM_LIMIT),
        name="feed_forward",
    )(normed, middle, w_up, w_down, vec, bias, cot_out, cot_pooled, ends)


def attend_tile_back(tile, proj, bounds, grad_mixed, grad_proj, grad_keys, grad_values):
    start = window_start(tile)
    rows, window = span(tile, QUERIES), pl.ds(start, WINDOW)
    mask = tile_mask(bounds, tile, start)
    for at in range(0, D, WIDE):
        here = slice(at, at + WIDE)
        queries = split_heads(scaled(proj[rows, here]))
        grads = split_heads(grad_mixed[rows, here])
        keys = proj[window, D + at : D + at + WIDE]
        values = proj[window, 2 * D + at : 2 * D + at + WIDE]
        probs = probabilities(keys, queries, mask)
        grad_probs = dot_nt(values, grads)
        along = jnp.sum(probs * grad_probs, 0, keepdims=True)
        grad_scores = (probs * (grad_probs - along)).astype(bf16)
        both = join_heads(dot_tn(grad_scores, keys)) * HEAD_DIM ** (-0.5)
        grad_proj[rows, here] = both.astype(bf16)
        grad_keys[window, here] += dot_nn(grad_scores, queries)
        grad_values[window, here] += dot_nn(probs.astype(bf16), grads)


def out_back_part(part, grad_middle, w_out, low_middle, grad_mixed, total):
    rows = span(part, 512)
    low = grad_middle[rows, :].astype(bf16)
    low_middle[rows, :] = low
    grad_mixed[rows, :] = dot_nt(low, w_out[...].reshape(D, D)).astype(bf16)
    return total + jnp.sum(low.astype(f32), 0, keepdims=True)


def finish_proj(grad_proj, grad_keys, grad_values, grad_small):
    grad_proj[:, D : 2 * D] = grad_keys[...].astype(bf16)
    grad_proj[:, 2 * D :] = grad_values[...].astype(bf16)
    grad_small[4:5, :] = jnp.sum(grad_proj[:, :D].astype(f32), 0, keepdims=True)
    grad_small[5:6, :] = jnp.sum(grad_proj[:, 2 * D :].astype(f32), 0, keepdims=True)


def project_back(normed_t, grad_proj, grad_qkv):
    def step(part, carry):
        place = span(part, D)
        grad_qkv[:, place] = dot_nn(normed_t[...], grad_proj[:, place]).astype(bf16)
        return carry

    lax.fori_loop(0, 3, step, 0)


def tokens_back(tokens, grad_proj, w_qkv, vec, grad_middle, grad_tokens, grad_small):
    def step(part, carry):
        gain, shift = carry
        rows = span(part, 512)
        grad = dot_nt(grad_proj[rows, :], w_qkv[...].reshape(D, 3 * D))
        unit, scale = normalise(tokens[rows, :].astype(f32))
        grad_tokens[rows, :] = grad_middle[rows, :] + normalise_back(grad, vec[0:1, :], unit, scale)
        return gain + jnp.sum(grad * unit, 0, keepdims=True), shift + jnp.sum(grad, 0, keepdims=True)

    zero = jnp.zeros((1, D), f32)
    gain, shift = lax.fori_loop(0, SEQ // 512, step, (zero, zero))
    grad_small[0:1, :] = gain
    grad_small[1:2, :] = shift


def backward_kernel(
    tokens,
    ends,
    w_qkv,
    w_out,
    vec,
    normed,
    proj,
    mixed,
    grad_middle,
    small,
    grad_tokens,
    grad_qkv,
    grad_out,
    grad_small,
    bounds,
    low_middle,
    grad_mixed,
    turned,
    grad_proj,
    grad_keys,
    grad_values,
):
    grad_small[...] = small[...]

    def part(index, total):
        return out_back_part(index, grad_middle, w_out, low_middle, grad_mixed, total)

    grad_small[6:7, :] = lax.fori_loop(0, SEQ // 512, part, jnp.zeros((1, D), f32))
    turned[...] = mixed[...].T
    grad_out[...] = dot_nn(turned[...], low_middle[...]).astype(bf16)
    caption_bounds(ends, bounds)
    grad_keys[...] = jnp.zeros_like(grad_keys)
    grad_values[...] = jnp.zeros_like(grad_values)

    def tile(index, carry):
        attend_tile_back(2 * index, proj, bounds, grad_mixed, grad_proj, grad_keys, grad_values)
        attend_tile_back(2 * index + 1, proj, bounds, grad_mixed, grad_proj, grad_keys, grad_values)
        return carry

    lax.fori_loop(0, SEQ // QUERIES // 2, tile, 0)
    finish_proj(grad_proj, grad_keys, grad_values, grad_small)
    turned[...] = normed[...].T
    project_back(turned, grad_proj, grad_qkv)
    tokens_back(tokens, grad_proj, w_qkv, vec, grad_middle, grad_tokens, grad_small)


def backward_call(tokens, ends, w_qkv, w_out, vec, normed, proj, mixed, grad_middle, small):
    shape = jax.ShapeDtypeStruct
    return pl.pallas_call(
        backward_kernel,
        out_shape=(
            shape((SEQ, D), f32),
            shape((D, 3 * D), bf16),
            shape((D, D), bf16),
            shape((16, D), f32),
        ),
        in_specs=vmem(1) + [SMEM] + vmem(8),
        out_specs=tuple(vmem(4)),
        scratch_shapes=[
            pltpu.VMEM((2, SEQ // QUERIES, GROUP * QUERIES), jnp.int32),
            pltpu.VMEM((SEQ, D), bf16),
            pltpu.VMEM((SEQ, D), bf16),
            pltpu.VMEM((D, SEQ), bf16),
            pltpu.VMEM((SEQ, 3 * D), bf16),
            pltpu.VMEM((SEQ, D), f32),
            pltpu.VMEM((SEQ, D), f32),
        ],
        compiler_params=pltpu.CompilerParams(vmem_limit_bytes=VMEM_LIMIT),
        name="backward",
    )(tokens, ends, w_qkv, w_out, vec, normed, proj, mixed, grad_middle, small)


class Place:
    def __init__(self, mesh_shape):
        line, face = mesh_shape["dp"] // 2, lax.axis_index("dp")
        cell = lax.axis_index("fsdp")
        self.line = line
        self.z, self.y = lax.div(face, 2), lax.rem(face, 2)
        self.x, self.c = lax.div(cell, 2), lax.rem(cell, 2)
        self.flat = face * 4 + cell
        self.fill()

    def fill(self):
        y, x, c = self.y, self.x, self.c
        self.near = (y + (1 - c) * (1 - 2 * y), x + c * (1 - 2 * x))
        self.far = (y + c * (1 - 2 * y), x + (1 - c) * (1 - 2 * x))
        self.cross = (1 - y, 1 - x)
        self.own = (y, x)

    def other(self):
        place = object.__new__(Place)
        place.line, place.z, place.y, place.x, place.c = self.line, self.z, self.y, self.x, 1 - self.c
        place.fill()
        return place

    def device(self, z, spot, c):
        return (z * 2 + spot[0], spot[1] * 2 + c)

    def sibling(self):
        return self.device(self.z, self.own, 1 - self.c)

    def along(self, step):
        return lax.rem(self.z + step, self.line)

    def peers(self):
        return [
            self.sibling(),
            self.device(self.z, self.near, self.c),
            self.device(self.z, self.far, self.c),
        ] + [self.device(self.along(step), self.own, self.c) for step in range(1, self.line)]


def greet(place):
    barrier = pltpu.get_barrier_semaphore()
    peers = place.peers()
    for peer in peers:
        pl.semaphore_signal(barrier, inc=1, device_id=peer, device_id_type=MESH)
    pl.semaphore_wait(barrier, len(peers))


def remote(source, target, send, recv, device):
    return pltpu.make_async_remote_copy(
        src_ref=source,
        dst_ref=target,
        send_sem=send,
        recv_sem=recv,
        device_id=device,
        device_id_type=MESH,
    )


def band(c, half):
    return pl.ds(pl.multiple_of(c * half, 128), half)


GATHER_SEMS = 20


class Gather:
    def __init__(self, place, shard, stage, whole, send, recv):
        self.place, self.shard, self.stage, self.whole = place, shard, stage, whole
        self.send, self.recv = send, recv
        self.rows, self.half = shard.shape[0], shard.shape[1] // 2

    def block(self, z, spot, c):
        return self.whole.at[z, spot[0], span(spot[1], 2 * self.rows), band(c, self.half)]

    def line(self, spot, c):
        return self.whole.at[:, spot[0], span(spot[1], 2 * self.rows), band(c, self.half)]

    def copy(self, ref, index, device, target=None):
        return remote(ref, ref if target is None else target, self.send.at[index], self.recv.at[index], device)

    def get(self, ref, index):
        self.copy(ref, index, self.place.sibling()).wait_recv()

    def swap_copy(self):
        p = self.place
        source = self.shard.at[:, band(1 - p.c, self.half)]
        return self.copy(source, 0, p.sibling(), self.stage.at[span(p.c, self.rows), :])

    def own_copies(self):
        p = self.place
        block = self.block(p.z, p.own, p.c)
        return [self.copy(block, step, p.device(p.along(step), p.own, p.c)) for step in range(1, p.line)]

    def on_copies(self):
        p = self.place
        ref = self.line(p.own, p.c)
        return [
            self.copy(ref, p.line, p.device(p.z, p.near, p.c)),
            self.copy(ref, p.line + 1, p.device(p.z, p.far, p.c)),
        ]

    def cross_copy(self):
        p = self.place
        return self.copy(self.line(p.near, p.c), p.line + 2, p.device(p.z, p.far, p.c))

    def hand_copy(self, group):
        p = self.place
        spot = (p.own, p.near, p.far, p.cross)[group]
        return self.copy(self.line(spot, p.c), p.line + 3 + group, p.sibling())

    def swap(self):
        p = self.place
        self.swap_copy().start()
        self.stage[span(p.c, self.rows), :] = self.shard[:, band(p.c, self.half)]

    def own(self):
        p = self.place
        self.get(self.stage.at[span(1 - p.c, self.rows), :], 0)
        self.whole[p.z, p.y, span(p.x, 2 * self.rows), band(p.c, self.half)] = self.stage[...].astype(bf16)
        for copy in self.own_copies():
            copy.start()

    def along_z(self):
        p = self.place
        for step in range(1, p.line):
            self.get(self.block(p.along(p.line - step), p.own, p.c), step)
        for copy in self.on_copies():
            copy.start()
        self.hand_copy(0).start()

    def from_near(self):
        p = self.place
        self.get(self.line(p.near, p.c), p.line)
        self.cross_copy().start()
        self.hand_copy(1).start()

    def from_far(self):
        p = self.place
        self.get(self.line(p.far, p.c), p.line + 1)
        self.hand_copy(2).start()
        self.get(self.line(p.cross, p.c), p.line + 2)
        self.hand_copy(3).start()

    def finish(self):
        o = self.place.other()
        for group, spot in enumerate((o.own, o.near, o.far, o.cross)):
            self.get(self.line(spot, o.c), o.line + 3 + group)

    def drain(self):
        self.swap_copy().wait_send()
        for copy in self.own_copies() + self.on_copies():
            copy.wait_send()
        self.cross_copy().wait_send()
        for group in range(4):
            self.hand_copy(group).wait_send()


class GatherPlanes(Gather):
    def pair(self, pair, spot, c):
        return self.whole.at[2 * pair : 2 * pair + 2, spot[0], span(spot[1], 2 * self.rows), band(c, self.half)]

    def on_copies(self, pair):
        p = self.place
        ref, index = self.pair(pair, p.own, p.c), p.line + 4 * pair
        return [
            self.copy(ref, index, p.device(p.z, p.near, p.c)),
            self.copy(ref, index + 1, p.device(p.z, p.far, p.c)),
        ]

    def cross_copy(self, pair):
        p = self.place
        return self.copy(self.pair(pair, p.near, p.c), p.line + 4 * pair + 2, p.device(p.z, p.far, p.c))

    def hand_copy(self, pair):
        p = self.place
        ref = self.whole.at[2 * pair : 2 * pair + 2, :, :, band(p.c, self.half)]
        return self.copy(ref, p.line + 4 * pair + 3, p.sibling())

    def along_z(self, pair):
        p = self.place
        for plane in (2 * pair, 2 * pair + 1):
            step = lax.rem(p.z - plane + p.line, p.line)

            @pl.when(step != 0)
            def _():
                self.get(self.block(plane, p.own, p.c), step)

        for copy in self.on_copies(pair):
            copy.start()

    def from_near(self, pair):
        p = self.place
        self.get(self.pair(pair, p.near, p.c), p.line + 4 * pair)
        self.cross_copy(pair).start()

    def from_far(self, pair):
        p = self.place
        self.get(self.pair(pair, p.far, p.c), p.line + 4 * pair + 1)
        self.get(self.pair(pair, p.cross, p.c), p.line + 4 * pair + 2)
        self.hand_copy(pair).start()

    def finish(self, pair):
        ref = self.whole.at[2 * pair : 2 * pair + 2, :, :, band(1 - self.place.c, self.half)]
        self.get(ref, self.place.line + 4 * pair + 3)

    def drain(self):
        self.swap_copy().wait_send()
        for copy in self.own_copies():
            copy.wait_send()
        for pair in range(self.place.line // 2):
            for copy in self.on_copies(pair):
                copy.wait_send()
            self.cross_copy(pair).wait_send()
            self.hand_copy(pair).wait_send()


class Spread:
    def __init__(self, place, tiles, send, recv):
        self.place, self.tiles, self.send, self.recv = place, tiles, send, recv

    def copy(self, ref, index, device):
        return remote(ref, ref, self.send.at[index], self.recv.at[index], device)

    def get(self, ref, index):
        self.copy(ref, index, self.place.sibling()).wait_recv()

    def chips(self, spot):
        return self.tiles.at[:, spot[0], spot[1]]

    def copies(self, stage):
        p = self.place
        far = p.device(p.z, p.far, p.c)
        if stage == 0:
            return [self.copy(self.tiles.at[p.z, p.y, p.x, p.c], 0, p.sibling())]
        if stage == 1:
            chip = self.tiles.at[p.z, p.y, p.x]
            return [self.copy(chip, step, p.device(p.along(step), p.own, p.c)) for step in range(1, p.line)]
        if stage == 2:
            return [
                self.copy(self.chips(p.own), p.line, p.device(p.z, p.near, p.c)),
                self.copy(self.chips(p.own), p.line + 1, far),
            ]
        return [self.copy(self.chips(p.near), p.line + 2, far)]

    def start(self, stage):
        for copy in self.copies(stage):
            copy.start()

    def first(self):
        self.start(0)

    def second(self):
        p = self.place
        self.get(self.tiles.at[p.z, p.y, p.x, 1 - p.c], 0)
        self.start(1)

    def third(self):
        p = self.place
        for step in range(1, p.line):
            self.get(self.tiles.at[p.along(p.line - step), p.y, p.x], step)
        self.start(2)

    def fourth(self):
        p = self.place
        self.get(self.chips(p.near), p.line)
        self.start(3)

    def finish(self):
        p = self.place
        self.get(self.chips(p.far), p.line + 1)
        self.get(self.chips(p.cross), p.line + 2)

    def drain(self):
        for stage in range(4):
            for copy in self.copies(stage):
                copy.wait_send()


def fill_tiles(place, tiles, olds, vectors, bias, moment_vec, moment_bias):
    here = (place.z, place.y, place.x, place.c)
    tiles[here] = jnp.zeros(tiles.shape[4:], tiles.dtype)
    tile = jnp.zeros(olds.shape[4:], f32)
    olds[here] = tile
    olds[here + (slice(0, 8), slice(0, vectors.shape[1]))] = vectors[...]
    olds[here + (slice(8, 9), slice(0, bias.shape[1]))] = bias[...]
    tiles[here] = olds[here].astype(tiles.dtype)
    olds[here] = tile
    olds[here + (slice(0, 8), slice(0, vectors.shape[1]))] = moment_vec[...]
    olds[here + (slice(8, 9), slice(0, bias.shape[1]))] = moment_bias[...]


def lay_out(tiles, first, size, out):
    lane = lax.broadcasted_iota(jnp.int32, (8, 128), 1)
    done = [jnp.zeros((8, 128), f32) for _ in range(out.shape[1] // 128)]
    line, count = tiles.shape[0], tiles.shape[0] * 8
    for index in range(count):
        tile = tiles[index // 8, index // 4 % 2, index // 2 % 2, index % 2].astype(f32)[first : first + 8]
        at, shift = divmod(index * size, 128)
        turned = pltpu.roll(tile, shift, 1) if shift else tile
        done[at] = jnp.where((lane >= shift) & (lane < shift + size), turned, done[at])
        if shift + size > 128:
            done[at + 1] = jnp.where(lane < shift + size - 128, turned, done[at + 1])
    for index, tile in enumerate(done):
        out[:, index * 128 : index * 128 + 128] = tile[: out.shape[0]]


class Reduce:
    def __init__(self, place, terms, other, far, got_far, near, got_near, line, got_line, whole, result, send, recv, mine=None):
        self.place, self.terms, self.other, self.mine = place, terms, other, mine
        self.far, self.got_far, self.near, self.got_near = far, got_far, near, got_near
        self.line, self.got_line, self.whole, self.result = line, got_line, whole, result
        self.send, self.recv = send, recv
        self.half = other.shape[-1]
        self.rows = whole.shape[0] // 2

    def copy(self, source, target, index, device):
        return remote(source, target, self.send.at[index], self.recv.at[index], device)

    def get(self, ref, index):
        self.copy(ref, ref, index, self.place.sibling()).wait_recv()

    def swap_copy(self):
        p = self.place
        return self.copy(self.terms.at[:, :, :, band(1 - p.c, self.half)], self.other, 0, p.sibling())

    def far_copy(self, group):
        p = self.place
        return self.copy(self.far.at[group], self.got_far.at[group], 1 + group, p.device(p.z, p.far, p.c))

    def near_copy(self):
        p = self.place
        return self.copy(self.near, self.got_near, 3, p.device(p.z, p.near, p.c))

    def line_copy(self, step):
        p = self.place
        target = p.device(p.along(step), p.own, p.c)
        return self.copy(self.line.at[step - 1], self.got_line.at[step - 1], 3 + step, target)

    def owner_copy(self):
        p = self.place
        source = self.whole.at[span(1 - p.c, self.rows), :]
        return self.copy(source, self.result.at[:, band(p.c, self.half)], 3 + p.line, p.sibling())

    def mine_copy(self):
        p = self.place
        source = self.terms.at[:, :, :, band(p.c, self.half)]
        return pltpu.make_async_copy(source, self.mine, self.send.at[4 + p.line])

    def swap(self):
        self.swap_copy().start()
        if self.mine is not None:
            self.mine_copy().start()

    def meet(self):
        self.get(self.other, 0)
        if self.mine is not None:
            self.mine_copy().wait()

    def pair(self, z, spot):
        rows = span(spot[1], 2 * self.rows)
        if self.mine is None:
            mine = self.terms[z, spot[0], rows, band(self.place.c, self.half)]
        else:
            mine = self.mine[z, spot[0], rows, :]
        return mine.astype(f32) + self.other[z, spot[0], rows, :].astype(f32)

    def to_far(self):
        p = self.place
        self.meet()
        for group, spot in enumerate((p.cross, p.far)):
            for z in range(p.line):
                self.far[group, z] = self.pair(z, spot).astype(bf16)
            self.far_copy(group).start()

    def to_near(self):
        p = self.place
        self.get(self.got_far.at[0], 1)
        for z in range(p.line):
            self.near[z] = (self.pair(z, p.near) + self.got_far[0, z].astype(f32)).astype(bf16)
        self.near_copy().start()

    def sum_own(self, z):
        return self.pair(z, self.place.own) + self.got_far[1, z].astype(f32) + self.got_near[z].astype(f32)

    def to_line(self):
        p = self.place
        self.get(self.got_far.at[1], 2)
        self.get(self.got_near, 3)
        self.send_line()

    def send_line(self):
        p = self.place
        for step in range(1, p.line):
            self.line[step - 1] = self.sum_own(p.along(step)).astype(bf16)
            self.line_copy(step).start()
        self.whole[...] = self.sum_own(p.z)

    def to_owner(self):
        p = self.place
        total = self.whole[...]
        for step in range(1, p.line):
            self.get(self.got_line.at[step - 1], 3 + step)
            total = total + self.got_line[step - 1].astype(f32)
        self.whole[...] = total
        self.owner_copy().start()
        self.result[:, band(p.c, self.half)] = self.whole[span(p.c, self.rows), :]

    def finish(self):
        p = self.place
        self.get(self.result.at[:, band(1 - p.c, self.half)], 3 + p.line)

    def drain(self):
        p = self.place
        self.swap_copy().wait_send()
        for group in range(2):
            self.far_copy(group).wait_send()
        self.near_copy().wait_send()
        for step in range(1, p.line):
            self.line_copy(step).wait_send()
        self.owner_copy().wait_send()


class ReducePlanes:
    def __init__(self, place, first, terms, other, far, got_far, near, got_near, line, got_line, whole, result, send, recv, mine=None):
        self.place, self.first, self.terms, self.other, self.mine = place, first, terms, other, mine
        self.far, self.got_far, self.near, self.got_near = far, got_far, near, got_near
        self.line, self.got_line, self.whole, self.result = line, got_line, whole, result
        self.send, self.recv = send, recv
        self.half = other.shape[-1]
        self.plane = first + place.c

    def copy(self, source, target, index, device):
        return remote(source, target, self.send.at[index], self.recv.at[index], device)

    def get(self, ref, index):
        self.copy(ref, ref, index, self.place.sibling()).wait_recv()

    def swap_copy(self):
        p = self.place
        return self.copy(self.terms.at[:, :, :, band(1 - p.c, self.half)], self.other, 0, p.sibling())

    def far_copy(self, group):
        p = self.place
        return self.copy(self.far.at[group], self.got_far.at[group], 1 + group, p.device(p.z, p.far, p.c))

    def near_copy(self):
        p = self.place
        return self.copy(self.near, self.got_near, 3, p.device(p.z, p.near, p.c))

    def line_copy(self):
        p = self.place
        step = lax.rem(self.plane - p.z + p.line, p.line)
        return self.copy(self.line, self.got_line.at[step - 1], 3 + step, p.device(self.plane, p.own, p.c))

    def owner_copy(self):
        p = self.place
        return self.copy(self.whole.at[1 - p.c], self.result, 3 + p.line, p.sibling())

    def mine_copy(self):
        p = self.place
        source = self.terms.at[:, :, :, band(p.c, self.half)]
        return pltpu.make_async_copy(source, self.mine, self.send.at[4 + p.line])

    def swap(self):
        self.swap_copy().start()
        if self.mine is not None:
            self.mine_copy().start()

    def meet(self):
        self.get(self.other, 0)
        if self.mine is not None:
            self.mine_copy().wait()

    def pair(self, spot):
        chip = spot[0] * 2 + spot[1]
        mine = self.terms[chip, :, :, band(self.place.c, self.half)] if self.mine is None else self.mine[chip]
        return mine.astype(f32) + self.other[chip].astype(f32)

    def to_far(self):
        p = self.place
        self.meet()
        for group, spot in enumerate((p.cross, p.far)):
            self.far[group] = self.pair(spot).astype(bf16)
            self.far_copy(group).start()

    def to_near(self):
        self.get(self.got_far.at[0], 1)
        self.near[...] = (self.pair(self.place.near) + self.got_far[0].astype(f32)).astype(bf16)
        self.near_copy().start()

    def to_line(self):
        p = self.place
        self.get(self.got_far.at[1], 2)
        self.get(self.got_near, 3)
        self.send_line(self.pair(p.own) + self.got_far[1].astype(f32) + self.got_near[...].astype(f32))

    def send_line(self, own):
        p = self.place

        @pl.when(p.z == self.plane)
        def _():
            self.whole[...] = own

        @pl.when(p.z != self.plane)
        def _():
            self.line[...] = own.astype(bf16)
            self.line_copy().start()

    def to_owner(self):
        p = self.place

        @pl.when(p.z == self.plane)
        def _():
            total = self.whole[...]
            for step in range(1, p.line):
                self.get(self.got_line.at[step - 1], 3 + step)
                total = total + self.got_line[step - 1].astype(f32)
            self.whole[...] = total
            self.owner_copy().start()
            self.result[...] = self.whole[p.c]

    def finish(self):
        p = self.place

        @pl.when(p.z == self.first + 1 - p.c)
        def _():
            self.get(self.result, 3 + p.line)

    def drain(self):
        p = self.place
        self.swap_copy().wait_send()
        for group in range(2):
            self.far_copy(group).wait_send()
        self.near_copy().wait_send()
        self.drain_line()

    def drain_line(self):
        p = self.place

        @pl.when(p.z == self.plane)
        def _():
            self.owner_copy().wait_send()

        @pl.when(p.z != self.plane)
        def _():
            self.line_copy().wait_send()


class ReduceStart(Reduce):
    def __init__(self, place, terms, other, far, got_far, near, own, send, recv):
        self.place, self.terms, self.other, self.mine = place, terms, other, None
        self.far, self.got_far, self.near, self.own = far, got_far, near, own
        self.send, self.recv = send, recv
        self.half = other.shape[-1]
        self.rows = own.shape[1] // 2

    def pass_sum(self):
        p = self.place
        self.get(self.got_far.at[0], 1)
        self.get(self.got_far.at[1], 2)
        for z in range(p.line):
            self.near[z] = (self.pair(z, p.near) + self.got_far[0, z].astype(f32)).astype(bf16)
            self.own[z] = self.pair(z, p.own) + self.got_far[1, z].astype(f32)

    def drain(self):
        self.swap_copy().wait_send()
        for group in range(2):
            self.far_copy(group).wait_send()


class ReducePlanesStart(ReducePlanes):
    def __init__(self, place, terms, other, far, got_far, near, own, send, recv):
        self.place, self.terms, self.other, self.mine = place, terms, other, None
        self.far, self.got_far, self.near, self.own = far, got_far, near, own
        self.send, self.recv = send, recv
        self.half = other.shape[-1]

    def pass_sum(self):
        p = self.place
        self.get(self.got_far.at[0], 1)
        self.get(self.got_far.at[1], 2)
        self.near[...] = (self.pair(p.near) + self.got_far[0].astype(f32)).astype(bf16)
        self.own[...] = self.pair(p.own) + self.got_far[1].astype(f32)

    def drain(self):
        self.swap_copy().wait_send()
        for group in range(2):
            self.far_copy(group).wait_send()


class ReduceRest(Reduce):
    def __init__(self, place, near, own, got_near, line, got_line, whole, result, send, recv):
        self.place, self.near, self.own, self.got_near = place, near, own, got_near
        self.line, self.got_line, self.whole, self.result = line, got_line, whole, result
        self.send, self.recv = send, recv
        self.half = near.shape[-1]
        self.rows = whole.shape[0] // 2

    def to_near(self):
        self.near_copy().start()

    def sum_own(self, z):
        return self.own[z] + self.got_near[z].astype(f32)

    def to_line(self):
        p = self.place
        self.get(self.got_near, 3)
        self.send_line()

    def drain(self):
        p = self.place
        self.near_copy().wait_send()
        for step in range(1, p.line):
            self.line_copy(step).wait_send()
        self.owner_copy().wait_send()


class ReducePlanesRest(ReducePlanes):
    def __init__(self, place, first, near, own, got_near, line, got_line, whole, result, send, recv):
        self.place, self.first, self.near, self.own, self.got_near = place, first, near, own, got_near
        self.line, self.got_line, self.whole, self.result = line, got_line, whole, result
        self.send, self.recv = send, recv
        self.half = near.shape[-1]
        self.plane = first + place.c

    def to_near(self):
        self.near_copy().start()

    def to_line(self):
        self.get(self.got_near, 3)
        self.send_line(self.own[...] + self.got_near[...].astype(f32))

    def drain(self):
        self.near_copy().wait_send()
        self.drain_line()


def reduce_scratch(line, rows, half, count):
    return [
        pltpu.VMEM((count, line, 2, 2 * rows, half), bf16),
        pltpu.VMEM((count, 2, line, rows, half), bf16),
        pltpu.VMEM((count, 2, line, rows, half), bf16),
        pltpu.VMEM((count, line, rows, half), bf16),
        pltpu.VMEM((count, line, rows, half), bf16),
        pltpu.VMEM((count, line - 1, rows, half), bf16),
        pltpu.VMEM((count, line - 1, rows, half), bf16),
        pltpu.VMEM((count, rows, half), f32),
    ]


def plane_scratch(line, rows, half, count):
    block = (2, rows, half)
    return [
        pltpu.VMEM((count, 4) + block, bf16),
        pltpu.VMEM((count, 2) + block, bf16),
        pltpu.VMEM((count, 2) + block, bf16),
        pltpu.VMEM((count,) + block, bf16),
        pltpu.VMEM((count,) + block, bf16),
        pltpu.VMEM((count,) + block, bf16),
        pltpu.VMEM((count, line - 1) + block, bf16),
        pltpu.VMEM((count,) + block, f32),
    ]


class AllSum:
    def __init__(self, place, value, slots, line, send, recv):
        self.place, self.value, self.slots, self.line = place, value, slots, line
        self.send, self.recv = send, recv

    def start(self, stage):
        p = self.place
        device = (p.sibling(), p.device(p.z, (p.y, 1 - p.x), p.c), p.device(p.z, (1 - p.y, p.x), p.c))[stage]
        self.copy = remote(self.value, self.slots.at[stage], self.send.at[stage], self.recv.at[stage], device)
        self.copy.start()

    def end(self, stage):
        self.copy.wait()
        self.value[...] = self.value[...] + self.slots[stage]

    def start_line(self):
        p = self.place
        self.line[p.z] = self.value[...]
        self.copies = [
            remote(self.line.at[p.z], self.line.at[p.z], self.send.at[2 + step], self.recv.at[2 + step],
                   p.device(p.along(step), p.own, p.c))
            for step in range(1, p.line)
        ]
        for copy in self.copies:
            copy.start()

    def end_line(self):
        p = self.place
        for step in range(1, p.line):
            ref = self.line.at[p.along(p.line - step)]
            remote(ref, ref, self.send.at[2 + step], self.recv.at[2 + step], p.sibling()).wait_recv()
        total = self.line[0]
        for z in range(1, p.line):
            total = total + self.line[z]
        self.value[...] = total
        for copy in self.copies:
            copy.wait_send()

    def next(self, stage):
        self.end(stage)
        if stage < 2:
            self.start(stage + 1)
        else:
            self.start_line()


def sum_scratch(line, rows):
    return [
        pltpu.VMEM((rows, D), f32),
        pltpu.VMEM((3, rows, D), f32),
        pltpu.VMEM((line, rows, D), f32),
        pltpu.SemaphoreType.DMA((2 + line,)),
        pltpu.SemaphoreType.DMA((2 + line,)),
    ]


def diagonal(size):
    return lax.broadcasted_iota(jnp.int32, (size, size), 0) == lax.broadcasted_iota(jnp.int32, (size, size), 1)


def to_column(row):
    return jnp.sum(jnp.where(diagonal(row.shape[1]), row, 0.0), 1, keepdims=True)


def to_row(column):
    return jnp.sum(jnp.where(diagonal(column.shape[0]), column, 0.0), 0, keepdims=True)


def total(values):
    return jnp.sum(jnp.sum(values, 1, keepdims=True), 0, keepdims=True)


def own_vectors(place, small, result, indices):
    size = result.shape[1]
    shape = (size, D)
    pick = lax.broadcasted_iota(jnp.int32, shape, 1) == place.flat * size + lax.broadcasted_iota(jnp.int32, shape, 0)
    row = lax.broadcasted_iota(jnp.int32, (8, size), 0)
    for index in indices:
        column = jnp.sum(jnp.where(pick, small[index : index + 1, :], 0.0), 1, keepdims=True)
        result = jnp.where(row == index, to_row(column), result)
    return result


def own_bias(place, small, size):
    per = D // size
    row, at = lax.div(place.flat, per), lax.rem(place.flat, per) * size
    shape = (FF // D, D)
    kept = lax.broadcasted_iota(jnp.int32, shape, 0) == row
    line = jnp.sum(jnp.where(kept, small[8 : 8 + FF // D, :], 0.0), 0, keepdims=True)
    shape = (size, D)
    pick = lax.broadcasted_iota(jnp.int32, shape, 1) == at + lax.broadcasted_iota(jnp.int32, shape, 0)
    return to_row(jnp.sum(jnp.where(pick, line, 0.0), 1, keepdims=True))


ROW_COUNTS = (D, D, D, FF)
SIZES = (3 * D * D, D * D, D * FF, FF * D)


def row_statistic(grad, old):
    mean = jnp.sum(grad * grad + square_eps, 1, keepdims=True) * (1.0 / grad.shape[1])
    return decay * to_column(old) + (1.0 - decay) * mean


def moment_of(grad, old):
    return decay * old + (1.0 - decay) * (grad * grad + square_eps)


def finish_kernel(*refs):
    refs = list(refs)

    def take(count):
        taken = refs[:count]
        del refs[:count]
        return taken

    large, grads, (grad_vec, grad_bias, stats), weights, (vectors, bias), rows, cols, (moment_vec, moment_bias) = (
        take(3), take(4), take(3), take(4), take(2), take(4), take(4), take(2)
    )
    out_large, out_grads, new_rows, new_cols, new_weights = take(3), take(4), take(4), take(4), take(4)
    out_vec, new_moment_vec, new_vec, out_bias, new_moment_bias, new_bias, clip_out = take(7)
    held, sems = take(3), take(1)[0]
    copies = []
    for index, count in enumerate((1, 1, 1)):
        size = held[index].shape[0] // count
        for part in range(count):
            piece, at = pl.ds(part * size, size), len(copies)
            copies.append(
                (
                    pltpu.make_async_copy(large[index].at[piece], held[index].at[piece], sems.at[0, at]),
                    pltpu.make_async_copy(held[index].at[piece], out_large[index].at[piece], sems.at[1, at]),
                )
            )
    for copy_in, _ in copies:
        copy_in.start()
    sums = stats[18:19, :]

    def one(index):
        return sums[:, index : index + 1]

    norm = one(17)
    at = 0
    col_rows, row_means = [], []
    for index in range(4):
        width = grads[index].shape[1]
        count = width // D
        sums_of = jnp.concatenate([stats[at + part : at + part + 1, :] for part in range(count)], 1)
        weighed = jnp.concatenate([stats[9 + at + part : 10 + at + part, :] for part in range(count)], 1)
        at += count
        col = decay * cols[index][...].reshape(1, width) + (1.0 - decay) * (sums_of * (1.0 / ROW_COUNTS[index]))
        new_cols[index][...] = col.reshape(width)
        col_rows.append(col)
        row_sum = decay * one(index) + (1.0 - decay) * (total(sums_of) * (1.0 / width))
        row_means.append(row_sum * (1.0 / ROW_COUNTS[index]))
        norm = norm + total(weighed / col) * row_means[index]
    for copy_in, copy_out in copies:
        copy_in.wait()
        copy_out.start()
    param_count = sum(SIZES) + 8 * D + FF
    clip = jnp.maximum(1.0, jnp.sqrt(norm * (1.0 / param_count)) * (1.0 / clip_limit))
    clip_out[...] = clip
    for index in range(4):
        grad = grads[index][...]
        out_grads[index][...] = grad
        row = row_statistic(grad, rows[index][...])
        new_rows[index][...] = to_row(row)
        scale = jnp.maximum(scale_floor, jnp.sqrt(one(4 + index) * (1.0 / SIZES[index])))
        update = grad * lax.rsqrt(row * col_rows[index] / row_means[index])
        new_weights[index][...] = weights[index][...] - (step_rate * scale / clip) * update
    lane = lax.broadcasted_iota(jnp.int32, (8, 1), 0)
    scale = jnp.zeros((8, 1), f32)
    for index in range(8):
        scale = jnp.where(lane == index, one(8 + index), scale)
    scale = jnp.maximum(scale_floor, jnp.sqrt(scale * (1.0 / D)))
    vec = grad_vec[...]
    moment = moment_of(vec, moment_vec[...])
    out_vec[...] = vec
    new_moment_vec[...] = moment
    new_vec[...] = vectors[...] - (step_rate * scale / clip) * (vec * lax.rsqrt(moment))
    scale = jnp.maximum(scale_floor, jnp.sqrt(one(16) * (1.0 / FF)))
    low = grad_bias[...]
    moment = moment_of(low, moment_bias[...])
    out_bias[...] = low
    new_moment_bias[...] = moment
    new_bias[...] = bias[...] - (step_rate * scale / clip) * (low * lax.rsqrt(moment))
    for _, copy_out in copies:
        copy_out.wait()


def finish_call(large, summed, weights, vectors, bias, rows, cols, moment_vec, moment_bias):
    shape = jax.ShapeDtypeStruct
    like = [shape(w.shape, f32) for w in weights]
    vec, low = shape(vectors.shape, f32), shape(bias.shape, f32)
    return pl.pallas_call(
        finish_kernel,
        out_shape=tuple(
            [shape(value.shape, value.dtype) for value in large]
            + like
            + [shape(r.shape, f32) for r in rows]
            + [shape(c.shape, f32) for c in cols]
            + like
            + [vec, vec, vec, low, low, low, shape((1, 1), f32)]
        ),
        in_specs=[pl.BlockSpec(memory_space=pl.ANY)] * 3 + vmem(23),
        out_specs=tuple([pl.BlockSpec(memory_space=pl.ANY)] * 3 + vmem(23)),
        scratch_shapes=[pltpu.VMEM(value.shape, value.dtype) for value in large] + [pltpu.SemaphoreType.DMA((2, 3))],
        compiler_params=pltpu.CompilerParams(vmem_limit_bytes=VMEM_LIMIT),
        name="finish",
    )(*large, *summed, *weights, vectors, bias, *rows, *cols, moment_vec, moment_bias)


def pooled_rows(ends, cot_pooled, parts):
    lane = lax.rem(lax.broadcasted_iota(jnp.int32, (1, 96), 1), 32)
    spot = jnp.full((1, 96), -1, jnp.int32)
    for index in range(ends.shape[1]):
        spot = jnp.where(lane == index, ends[0, index], spot)
    left = cot_pooled[0]
    parts[...] = jnp.zeros_like(parts)
    for index in range(3):
        low = left.astype(bf16)
        parts[32 * index : 32 * index + left.shape[0], :] = low
        left = left - low.astype(f32)
    return spot


def attend_group(tile, group, proj, masks, mixed):
    start = window_start(tile)
    rows, window, at = span(tile, QUERIES), pl.ds(start, WINDOW), group * D
    mask = masks[tile]
    queries = split_heads(scaled(proj[rows, at : at + WIDE]))
    keys = proj[window, at + WIDE : at + 2 * WIDE]
    values = proj[window, at + 2 * WIDE : at + D]
    probs = probabilities(keys, queries, mask).astype(bf16)
    return rows, join_heads(dot_tn(probs, values)).astype(bf16)


def feed_rows(rows, cols, normed, up, down, bias, low_final, hidden, grad_pre, final, grad_normed):
    root = 0.7978845608028654
    cube = 0.044715
    pre = dot_nn(normed[rows, :], up()) + bias[0:1, cols]
    square = pre * pre
    half = 0.5 + 0.5 * jnp.tanh(pre * (root + (root * cube) * square))
    act = pre * half
    slope = half + act * ((1.0 - half) * (2.0 * root + (6.0 * root * cube) * square))
    act = act.astype(bf16)
    hidden[rows, :] = act
    final[rows, :] = final[rows, :] + dot_nn(act, down())
    back = (dot_nt(low_final[rows, :], down()) * slope).astype(bf16)
    grad_pre[rows, :] = back
    grad_normed[rows, :] = grad_normed[rows, :] + dot_nt(back, up())
    return jnp.sum(back.astype(f32), 0, keepdims=True)


def front_kernel(mesh_shape, *refs):
    refs = list(refs)

    def take(count):
        taken = refs[:count]
        del refs[:count]
        return taken

    tokens, ends, cot_out, cot_pooled, w_qkv, w_out, w_up, w_down = take(8)
    vectors, bias, moment_vec, moment_bias = take(4)
    out_both, out_normed, out_proj, out_mixed, out_tokens, out_middle, out_up, out_down, out_masks = take(9)
    vec, moments, pooled, grad_small, near_up, own_up, near_down, own_down = take(8)
    shards, stage, stage_down, weights, all_down, tiles, olds, all_bias = take(8)
    normed, proj, mixed, middle, normed_two, final, grad_middle, grad_normed, normed_t = take(9)
    bounds, masks, parts = take(3)
    up_scratch, down_scratch = take(3), take(3)
    send, recv, sum_send, sum_recv, tile_send, tile_recv, old_send, old_recv, out_sems = take(9)

    place = Place(mesh_shape)
    line = place.line
    cut = (line, 2, D // (2 * line), D)
    copies = {}

    def leave(name, source, target):
        copies[name] = pltpu.make_async_copy(source, target, out_sems.at[len(copies)])
        copies[name].start()

    spread = Spread(place, tiles, tile_send, tile_recv)
    old_spread = Spread(place, olds, old_send, old_recv)

    def gather_of(index, first, last):
        whole, half = slice(first * D, last * D), slice(first * D // 2, last * D // 2)
        return Gather(
            place, shards.at[:, whole], stage.at[:, half], weights.at[:, :, :, whole], send.at[index], recv.at[index]
        )

    g0, g1, g2, u0, u1 = (gather_of(*given) for given in ((0, 0, 1), (1, 1, 2), (2, 2, 3), (3, 3, 6), (4, 6, 8)))
    down = GatherPlanes(place, w_down, stage_down, all_down, send.at[5], recv.at[5])

    def begin():
        fill_tiles(place, tiles, olds, vectors, bias, moment_vec, moment_bias)
        greet(place)

    def lay_qkv():
        for group in range(3):
            for part in range(3):
                at = group * D + part * WIDE
                shards[:, at : at + WIDE] = w_qkv[:, part * D + group * WIDE : part * D + (group + 1) * WIDE]

    def lay_rest():
        shards[:, 3 * D : 4 * D] = w_out[...]
        shards[:, 4 * D :] = w_up[...]

    def cotangent():
        spot = pooled_rows(ends, cot_pooled, parts)
        caption_bounds(ends, bounds)

        def mask_of(tile, carry):
            masks[tile] = tile_mask(bounds, tile, window_start(tile))
            return carry

        lax.fori_loop(0, SEQ // QUERIES, mask_of, 0)
        leave("masks", masks, out_masks)

        def rows_of(part, carry):
            rows = span(part, 256)
            place_of = part * 256 + lax.broadcasted_iota(jnp.int32, (256, 96), 0)
            picked = dot_nn(jnp.where(place_of == spot, 1.0, 0.0).astype(bf16), parts[...])
            grad_middle[rows, :] = cot_out[rows, :].astype(f32) + picked
            return carry

        lax.fori_loop(0, SEQ // 256, rows_of, 0)

    def norm_tokens():
        lay_out(tiles, 0, vectors.shape[1], vec)
        first_norm(tokens, vec, normed)
        leave("normed", normed, out_normed)

    def project_group(group):
        at = group * D
        here = slice(group * WIDE, (group + 1) * WIDE)
        shift = jnp.concatenate([vec[4:5, here], jnp.zeros((1, WIDE), f32), vec[5:6, here]], 1)

        def half(part, carry):
            rows = span(part, 512)
            weight = weights[:, :, :, at : at + D].reshape(D, D)
            proj[rows, at : at + D] = (dot_nn(normed[rows, :], weight) + shift).astype(bf16)
            return carry

        lax.fori_loop(0, SEQ // 512, half, 0)

    def attend(group, *calls):
        here = slice(group * WIDE, (group + 1) * WIDE)
        each = SEQ // QUERIES // 4

        def tile(index, carry):
            for inner in range(4):
                rows, value = attend_group(4 * index + inner, group, proj, masks, mixed)
                mixed[rows, here] = value

            @pl.when(index == each // 2 - 1)
            def _():
                for call in calls:
                    call()

            return carry

        lax.fori_loop(0, each, tile, 0)

    def middle_rows():
        leave("both", weights.at[:, :, :, 0 : 4 * D], out_both)
        leave("mixed", mixed, out_mixed)
        leave("proj", proj, out_proj)

        def part(index, carry):
            middle_part(index, tokens, mixed, weights.at[:, :, :, 3 * D : 4 * D], vec, middle, normed_two)
            return carry

        lax.fori_loop(0, SEQ // 512, part, 0)

    hidden, grad_pre, low_final = proj.at[:, 0:D], proj.at[:, D : 2 * D], proj.at[:, 2 * D :]

    def prepare():
        normed_t[...] = normed_two[...].T
        final[...] = middle[...] + vec[7:8, :]
        grad_normed[...] = jnp.zeros_like(grad_normed)
        grad_small[...] = jnp.zeros_like(grad_small)
        lay_out(tiles, 8, bias.shape[1], all_bias)
        for name in ("normed", "both", "mixed", "proj"):
            copies[name].wait()
        u0.drain()
        low_final[...] = grad_middle[...].astype(bf16)
        grad_small[7:8, :] = jnp.sum(low_final[...].astype(f32), 0, keepdims=True)

    up_sum = ReduceStart(place, weights.at[:, :, :, 0 : 2 * D], *up_scratch, near_up, own_up, sum_send.at[0], sum_recv.at[0])
    down_sum = ReducePlanesStart(
        place, weights.at[:, :, :, 2 * D : 4 * D], *down_scratch, near_down, own_down, sum_send.at[1], sum_recv.at[1]
    )

    def chunk_copies(chunk):
        which = chunk - 2
        return (
            pltpu.make_async_copy(
                weights.at[:, :, :, span(2 * chunk, D)], out_up.at[:, :, :, span(which, D)], out_sems.at[10 + which]
            ),
            pltpu.make_async_copy(
                weights.at[:, :, :, span(2 * chunk + 1, D)], out_down.at[:, :, :, span(which, D)], out_sems.at[12 + which]
            ),
        )

    def feed(chunk, carry):
        later = chunk // 2

        def when(value, *calls):
            @pl.when(chunk == value)
            def _():
                for call in calls:
                    call()

        def up_weight():
            return columns(weights, 4 + chunk, D)

        def down_weight():
            return all_down[chunk].reshape(D, D)

        total = jnp.zeros((1, D), f32)
        for block in range(SEQ // 512):
            total = total + feed_rows(
                pl.ds(block * 512, 512), span(chunk, D), normed_two, up_weight, down_weight, all_bias,
                low_final, hidden, grad_pre, final, grad_normed,
            )
        grad_small[pl.ds(8 + chunk, 1), :] = total
        when(0, u1.from_near)
        when(1, u1.from_far, functools.partial(down.from_far, 1))
        when(2, down_sum.to_far, up_sum.to_far)
        when(3, down_sum.pass_sum)
        weights[:, :, :, span(chunk + 2 + later * (chunk - 1), D)] = dot_tn(hidden[...], low_final[...]).astype(bf16).reshape(cut)
        when(1, down_sum.swap, u1.finish)
        when(3, up_sum.pass_sum)
        weights[:, :, :, span(chunk + later * chunk, D)] = dot_nn(normed_t[...], grad_pre[...]).astype(bf16).reshape(cut)
        when(0, functools.partial(down.from_near, 1), old_spread.finish)
        when(1, functools.partial(down.finish, 1), up_sum.swap, u1.drain)

        @pl.when(chunk >= 2)
        def _():
            for copy in chunk_copies(chunk):
                copy.start()

        return carry

    def last_copies(part):
        rows = span(part, 256)
        return (
            pltpu.make_async_copy(hidden.at[rows, :], out_tokens.at[rows, :], out_sems.at[14 + part]),
            pltpu.make_async_copy(grad_middle.at[rows, :], out_middle.at[rows, :], out_sems.at[18 + part]),
        )

    def last():
        def back(part, carry):
            gain, shift = carry
            rows = span(part, 256)
            unit, scale = normalise(middle[rows, :])
            grad = grad_normed[rows, :]
            grad_middle[rows, :] = grad_middle[rows, :] + normalise_back(grad, vec[2:3, :], unit, scale)
            hidden[rows, :] = final[rows, :].astype(bf16)
            for copy in last_copies(part):
                copy.start()
            return gain + jnp.sum(grad * unit, 0, keepdims=True), shift + jnp.sum(grad, 0, keepdims=True)

        zero = jnp.zeros((1, D), f32)
        gain, shift = lax.fori_loop(0, SEQ // 256, back, (zero, zero))
        grad_small[2:3, :] = gain
        grad_small[3:4, :] = shift
        lay_out(olds, 8, bias.shape[1], all_bias)
        moments[...] = jnp.ones_like(moments)
        lay_out(olds, 0, vectors.shape[1], moments.at[0:8, :])
        for index in range(FF // D):
            moments[8 + index : 9 + index, :] = all_bias[0:1, index * D : index * D + D]
        for index in range(ends.shape[1]):
            pooled[0, index : index + 1, :] = final[pl.ds(ends[0, index], 1), :]
        for user in (down, old_spread, up_sum, down_sum):
            user.drain()
        copies["masks"].wait()
        for part in range(4):
            for copy in last_copies(part):
                copy.wait()
        for chunk in (2, 3):
            for copy in chunk_copies(chunk):
                copy.wait()

    begin()
    spread.first()
    lay_qkv()
    g0.swap()
    g1.swap()
    g2.swap()
    lay_rest()
    u0.swap()
    down.swap()
    u1.swap()
    cotangent()
    spread.second()
    g0.own()
    g1.own()
    u0.own()
    spread.third()
    spread.fourth()
    g0.along_z()
    spread.finish()
    norm_tokens()
    g1.along_z()
    g0.from_near()
    g1.from_near()
    g2.own()
    u0.along_z()
    g0.from_far()
    down.own()
    g1.from_far()
    spread.drain()
    g0.finish()
    project_group(0)
    g1.finish()
    old_spread.first()
    attend(0, g2.along_z, old_spread.second)
    project_group(1)
    attend(1)
    g2.from_near()
    u0.from_near()
    g2.from_far()
    down.along_z(0)
    u1.own()
    g2.finish()
    project_group(2)
    attend(2)
    u0.from_far()
    old_spread.third()
    down.from_near(0)
    g0.drain()
    g1.drain()
    g2.drain()
    u0.finish()
    middle_rows()
    u1.along_z()
    down.along_z(1)
    down.from_far(0)
    old_spread.fourth()
    prepare()
    down.finish(0)
    lax.fori_loop(0, FF // D, feed, 0)
    last()


def front_call(
    mesh_shape, tokens, ends, cot_out, cot_pooled, w_qkv, w_out, w_up, w_down, vectors, bias, moment_vec, moment_bias
):
    shape = jax.ShapeDtypeStruct
    line = mesh_shape["dp"] // 2
    rows, tall = w_up.shape[0], w_down.shape[0]
    low, full = pltpu.VMEM((SEQ, D), bf16), pltpu.VMEM((SEQ, D), f32)
    dma = pltpu.SemaphoreType.DMA
    return pl.pallas_call(
        functools.partial(front_kernel, mesh_shape),
        out_shape=(
            shape((line, 2, 4 * rows, 4 * D), bf16),
            shape((SEQ, D), bf16),
            shape((SEQ, 3 * D), bf16),
            shape((SEQ, D), bf16),
            shape((SEQ, D), bf16),
            shape((SEQ, D), f32),
            shape((line, 2, 4 * rows, 2 * D), bf16),
            shape((4, 2, tall, 2 * D), bf16),
            shape((SEQ // QUERIES, WINDOW, GROUP * QUERIES), f32),
            shape((8, D), f32),
            shape((16, D), f32),
            shape((1, ends.shape[1], D), f32),
            shape((16, D), f32),
            shape((line, 2 * rows, D), bf16),
            shape((line, 2 * rows, D), f32),
            shape((2, tall, D), bf16),
            shape((2, tall, D), f32),
        ),
        in_specs=vmem(1) + [SMEM] + vmem(10),
        out_specs=tuple([pl.BlockSpec(memory_space=pl.ANY)] * 9 + vmem(8)),
        scratch_shapes=[
            pltpu.VMEM((rows, 8 * D), f32),
            pltpu.VMEM((2 * rows, 4 * D), f32),
            pltpu.VMEM((2 * tall, D // 2), f32),
            pltpu.VMEM((line, 2, 4 * rows, 8 * D), bf16),
            pltpu.VMEM((line, 2, 4 * tall, D), bf16),
            pltpu.VMEM((line, 2, 2, 2, 16, 128), bf16),
            pltpu.VMEM((line, 2, 2, 2, 16, 128), f32),
            pltpu.VMEM((1, FF), f32),
            low,
            pltpu.VMEM((SEQ, 3 * D), bf16),
            low,
            full,
            low,
            full,
            full,
            full,
            pltpu.VMEM((D, SEQ), bf16),
            pltpu.VMEM((2, SEQ // QUERIES, GROUP * QUERIES), jnp.int32),
            pltpu.VMEM((SEQ // QUERIES, WINDOW, GROUP * QUERIES), f32),
            pltpu.VMEM((96, D), bf16),
            pltpu.VMEM((line, 2, 4 * rows, D), bf16),
            pltpu.VMEM((2, line, 2 * rows, D), bf16),
            pltpu.VMEM((2, line, 2 * rows, D), bf16),
            pltpu.VMEM((4, 2, tall, D), bf16),
            pltpu.VMEM((2, 2, tall, D), bf16),
            pltpu.VMEM((2, 2, tall, D), bf16),
            dma((6, 3 * line)),
            dma((6, 3 * line)),
            dma((2, 3)),
            dma((2, 3)),
            dma((line + 3,)),
            dma((line + 3,)),
            dma((line + 3,)),
            dma((line + 3,)),
            dma((22,)),
        ],
        compiler_params=pltpu.CompilerParams(
            vmem_limit_bytes=FRONT_LIMIT, collective_id=0, has_side_effects=True
        ),
        name="front",
    )(tokens, ends, cot_out, cot_pooled, w_qkv, w_out, w_up, w_down, vectors, bias, moment_vec, moment_bias)


FRONT_LIMIT = 62 * 1024 * 1024


def attend_group_back(tile, group, proj, masks, grad_mixed):
    start = window_start(tile)
    rows, window, at = span(tile, QUERIES), pl.ds(start, WINDOW), group * D
    mask = masks[tile]
    queries = split_heads(scaled(proj[rows, at : at + WIDE]))
    grads = split_heads(grad_mixed[rows, group * WIDE : (group + 1) * WIDE])
    keys = proj[window, at + WIDE : at + 2 * WIDE]
    values = proj[window, at + 2 * WIDE : at + D]
    probs = probabilities(keys, queries, mask)
    grad_probs = dot_nt(values, grads)
    along = jnp.sum(probs * grad_probs, 0, keepdims=True)
    grad_scores = (probs * (grad_probs - along)).astype(bf16)
    both = join_heads(dot_tn(grad_scores, keys)) * HEAD_DIM ** (-0.5)
    return rows, window, both.astype(bf16), dot_nn(grad_scores, queries), dot_nn(probs.astype(bf16), grads)


def rear_kernel(mesh_shape, *refs):
    refs = list(refs)

    def take(count):
        taken = refs[:count]
        del refs[:count]
        return taken

    from_tokens, ends, from_both, vec, moments, small = take(6)
    from_proj, from_normed, from_mixed, from_middle, from_up, from_down, from_masks = take(7)
    near_up, own_up, near_down, own_down = take(4)
    weights, (vectors, bias), rows = take(4), take(2), take(4)
    out_tokens, grads, (grad_vec, grad_bias, stats) = take(1)[0], take(4), take(3)
    proj, spare, turned, low_middle, grad_mixed, grad_keys, grad_values, grad_middle, masks, w_both, tokens = take(11)
    term_out, term_groups, part_out, part_groups = take(4)
    up_rest, down_rest = take(4), take(4)
    up_mine, up_scratch, down_mine, down_scratch = take(1)[0], take(8), take(1)[0], take(8)
    scratch = take(8)
    early, late, send, recv, sems, load_sems = take(5), take(5), *take(4)
    place = Place(mesh_shape)
    line = place.line
    cut = (line, 2, D // (2 * line), D)
    def load(index, source, target):
        size = target.shape[0] // 4
        return [
            pltpu.make_async_copy(source.at[pl.ds(part * size, size)], target.at[pl.ds(part * size, size)], load_sems.at[index, part])
            for part in range(4)
        ]

    def wait_for(index):
        for copy in loads[index]:
            copy.wait()

    out_part, qkv_part = slice(3 * D, 4 * D), slice(0, 3 * D)
    loads = [
        load(0, from_middle, grad_middle),
        load(1, from_both.at[:, :, :, out_part], w_both.at[:, :, :, out_part]),
        load(2, from_mixed, spare),
        load(3, from_proj, proj),
        load(4, from_masks, masks),
        load(5, from_both.at[:, :, :, qkv_part], w_both.at[:, :, :, qkv_part]),
        load(6, from_tokens, tokens),
    ]
    normed_copy = pltpu.make_async_copy(from_normed, spare, sems.at[0])
    token_copies = [
        pltpu.make_async_copy(grad_middle.at[at : at + 512, :], out_tokens.at[at : at + 512, :], sems.at[1 + at // 512])
        for at in range(0, SEQ, 512)
    ]

    half_up = grads[2].at[:, 0 : 2 * D], grads[2].at[:, 2 * D :]
    u0 = ReduceRest(place, near_up, own_up, *up_rest, half_up[0], send.at[0], recv.at[0])
    d0 = ReducePlanesRest(place, 0, near_down, own_down, *down_rest, grads[3], send.at[1], recv.at[1])
    u1 = Reduce(place, from_up, *[ref.at[0] for ref in up_scratch], half_up[1], send.at[2], recv.at[2], up_mine)
    d1 = ReducePlanes(
        place, 2, from_down, *[ref.at[0] for ref in down_scratch], grads[3], send.at[3], recv.at[3], down_mine
    )

    def attention_of(index):
        term, part = (term_groups.at[index], part_groups.at[index]) if index < 3 else (term_out, part_out)
        return Reduce(place, term, *[ref.at[index] for ref in scratch], part, send.at[4 + index], recv.at[4 + index])

    g0, g1, g2, out = (attention_of(index) for index in range(4))
    early_sum, late_sum = AllSum(place, *early), AllSum(place, *late)
    first, second = early[0], late[0]
    local = LocalTerms(weights, rows)

    def begin():
        for copies in loads:
            for copy in copies:
                copy.start()
        greet(place)

    def prepare():
        first[...] = jnp.zeros_like(first)
        first[0:16, :] = small[...]
        second[...] = jnp.zeros_like(second)
        wait_for(0)
        wait_for(1)

    def out_back():
        w_out = w_both.at[:, :, :, 3 * D :]

        def out_part(part, total):
            return out_back_part(part, grad_middle, w_out, low_middle, grad_mixed, total)

        first[6:7, :] = lax.fori_loop(0, SEQ // 512, out_part, jnp.zeros((1, D), f32))

    def out_grad():
        wait_for(2)
        turned[...] = spare[...].T
        normed_copy.start()

        def third(part, carry):
            term = dot_nn(turned[...], low_middle[:, span(part, WIDE)]).astype(bf16)
            term_out[:, :, :, span(part, WIDE)] = term.reshape(cut[:3] + (WIDE,))
            return carry

        lax.fori_loop(0, 3, third, 0)
        normed_copy.wait()
        turned[...] = spare[...].T
        wait_for(3)
        wait_for(4)

    def tiles(group, *calls):
        at = group * D
        each = SEQ // QUERIES // 4
        grad_keys[...] = jnp.zeros_like(grad_keys)
        grad_values[...] = jnp.zeros_like(grad_values)

        def tile(index, carry):
            done = [attend_group_back(4 * index + inner, group, proj, masks, grad_mixed) for inner in range(4)]
            for where, window, query, key, value in done:
                proj[where, at : at + WIDE] = query
                grad_keys[window, :] += key
                grad_values[window, :] += value

            @pl.when(index == each // 2 - 1)
            def _():
                for call in calls:
                    call()

            return carry

        lax.fori_loop(0, each, tile, 0)

    def group_grad(group):
        at = group * D
        here = slice(group * WIDE, (group + 1) * WIDE)
        proj[:, at + WIDE : at + 2 * WIDE] = grad_keys[...].astype(bf16)
        proj[:, at + 2 * WIDE : at + D] = grad_values[...].astype(bf16)

        def third(part, carry):
            term = dot_nn(turned[...], proj[:, span(3 * group + part, WIDE)]).astype(bf16)
            term_groups[group, :, :, :, span(part, WIDE)] = term.reshape(cut[:3] + (WIDE,))
            return carry

        lax.fori_loop(0, 3, third, 0)
        first[4:5, here] = jnp.sum(proj[:, at : at + WIDE].astype(f32), 0, keepdims=True)
        first[5:6, here] = jnp.sum(proj[:, at + 2 * WIDE : at + D].astype(f32), 0, keepdims=True)

    def tokens_part(part):
        if part == 0:
            wait_for(5)
            wait_for(6)

        def quarter(index, carry):
            where = span(2 * part + index, 256)
            grad = dot_nt(proj[where, :], w_both[:, :, :, 0 : 3 * D].reshape(D, 3 * D))
            unit, scale = normalise(tokens[where, :].astype(f32))
            grad_middle[where, :] = grad_middle[where, :] + normalise_back(grad, vec[0:1, :], unit, scale)
            second[0:1, :] = second[0:1, :] + jnp.sum(grad * unit, 0, keepdims=True)
            second[1:2, :] = second[1:2, :] + jnp.sum(grad, 0, keepdims=True)
            return carry

        lax.fori_loop(0, 2, quarter, 0)
        token_copies[part].start()

    def feed_terms():
        local.matrix(2, grads[2], first, 16)
        local.matrix(3, grads[3], first, 24)
        local.rest(vectors, bias)
        first[26:27, :] = local.sums

    def out_terms():
        grads[1][...] = part_out[...]
        local.matrix(1, grads[1], first, 27)

    def qkv_terms():
        for index in range(3):
            for piece in range(3):
                at = piece * D + index * WIDE
                grads[0][:, at : at + WIDE] = part_groups[index, :, piece * WIDE : (piece + 1) * WIDE]
        local.matrix(0, grads[0], second, 2)

    def squared_updates(grad, moment):
        update = grad * lax.rsqrt(moment_of(grad, moment))
        return total(update * update)

    def early_results():
        grad_vec[...] = own_vectors(place, first, jnp.zeros(vectors.shape, f32), range(2, 8))
        grad_bias[...] = own_bias(place, first, bias.shape[1])
        stats[...] = jnp.zeros_like(stats)
        stats[3:4, :] = first[27:28, :]
        stats[4:8, :] = first[16:20, :]
        stats[8:9, :] = first[24:25, :]
        stats[12:13, :] = first[28:29, :]
        stats[13:17, :] = first[20:24, :]
        stats[17:18, :] = first[25:26, :]
        lane = lax.broadcasted_iota(jnp.int32, (1, D), 1)
        norm = squared_updates(first[0:16, :], moments[...])
        stats[18:19, :] = jnp.where(lane == 17, norm, first[26:27, :])

    def last():
        grad_vec[...] = own_vectors(place, second, grad_vec[...], range(2))
        stats[0:3, :] = second[2:5, :]
        stats[9:12, :] = second[5:8, :]
        lane = lax.broadcasted_iota(jnp.int32, (1, D), 1)
        norm = squared_updates(second[0:2, :], moments[0:2, :])
        stats[18:19, :] = jnp.where(lane == 17, stats[18:19, :] + norm, stats[18:19, :])
        for copy in token_copies:
            copy.wait()

    begin()
    u1.swap()
    u0.to_near()
    d0.to_near()
    prepare()
    out_back()
    u1.to_far()
    out_grad()
    out.swap()
    tiles(0, u0.to_line, out.to_far, d0.to_line, d1.swap)
    u1.to_near()
    out.to_near()
    d1.to_far()
    group_grad(0)
    tiles(1, u0.to_owner)
    u0.finish()
    out.to_line()
    u1.to_line()
    g0.swap()
    group_grad(1)
    g1.swap()
    d1.to_near()
    tiles(2, g0.to_far, g1.to_far, d1.to_line, d1.to_owner, d1.finish)
    out.to_owner()
    d0.to_owner()
    u1.to_owner()
    d0.finish()
    group_grad(2)
    g0.to_near()
    out.finish()
    g1.to_near()
    g2.swap()
    out_terms()
    u1.finish()
    feed_terms()
    g2.to_far()
    early_sum.start(0)
    g0.to_line()
    g1.to_line()
    tokens_part(0)
    g2.to_near()
    early_sum.next(0)
    tokens_part(1)
    g0.to_owner()
    g1.to_owner()
    early_sum.next(1)
    g2.to_line()
    g0.finish()
    g1.finish()
    early_sum.next(2)
    g2.to_owner()
    g2.finish()
    qkv_terms()
    late_sum.start(0)
    u0.drain()
    d0.drain()
    u1.drain()
    late_sum.next(0)
    d1.drain()
    out.drain()
    late_sum.next(1)
    g0.drain()
    g1.drain()
    early_sum.end_line()
    late_sum.next(2)
    g2.drain()
    early_results()
    late_sum.end_line()
    last()


class LocalTerms:
    def __init__(self, weights, rows):
        self.weights, self.rows = weights, rows
        self.lane = lax.broadcasted_iota(jnp.int32, (1, D), 1)
        self.sums = jnp.zeros((1, D), f32)

    def matrix(self, index, source, value, at):
        grad = source[...]
        row = row_statistic(grad, self.rows[index][...])
        square = grad * grad
        line = jnp.sum(square + square_eps, 0, keepdims=True)
        weighed = jnp.sum(square * (1.0 / row), 0, keepdims=True)
        count = grad.shape[1] // D
        for part in range(count):
            value[at + part : at + part + 1, :] = line[:, part * D : part * D + D]
            value[at + count + part : at + count + part + 1, :] = weighed[:, part * D : part * D + D]

    def rest(self, vectors, bias):
        for index in range(4):
            weight = self.weights[index][...]
            old = jnp.sum(self.rows[index][...], 1, keepdims=True)
            self.sums = jnp.where(self.lane == index, old, self.sums)
            self.sums = jnp.where(self.lane == 4 + index, total(weight * weight), self.sums)
        squares = jnp.sum(vectors[...] * vectors[...], 1, keepdims=True)
        for index in range(8):
            self.sums = jnp.where(self.lane == 8 + index, squares[index : index + 1, :], self.sums)
        self.sums = jnp.where(self.lane == 16, total(bias[...] * bias[...]), self.sums)


def rear_call(
    mesh_shape, tokens, ends, w_both, vec, moments, small, proj, normed, mixed, middle, terms, sums, weights, vectors, bias, rows
):
    shape = jax.ShapeDtypeStruct
    line = mesh_shape["dp"] // 2
    low = pltpu.VMEM((SEQ, D), bf16)
    tall, deep = weights[2].shape[0], weights[3].shape[0]
    cut = (line, 2, 4 * tall)
    far = pl.BlockSpec(memory_space=pl.ANY)
    return pl.pallas_call(
        functools.partial(rear_kernel, mesh_shape),
        out_shape=(shape((SEQ, D), f32),)
        + tuple(shape(w.shape, f32) for w in weights)
        + (shape(vectors.shape, f32), shape(bias.shape, f32), shape((24, D), f32)),
        in_specs=[far, SMEM, far] + vmem(3) + [far] * 7 + vmem(14),
        out_specs=tuple([pl.BlockSpec(memory_space=pl.ANY)] + vmem(7)),
        scratch_shapes=[
            pltpu.VMEM((SEQ, 3 * D), bf16),
            low,
            pltpu.VMEM((D, SEQ), bf16),
            low,
            low,
            pltpu.VMEM((SEQ, WIDE), f32),
            pltpu.VMEM((SEQ, WIDE), f32),
            pltpu.VMEM((SEQ, D), f32),
            pltpu.VMEM((SEQ // QUERIES, WINDOW, GROUP * QUERIES), f32),
            pltpu.VMEM(w_both.shape, bf16),
            low,
            pltpu.VMEM(cut + (D,), bf16),
            pltpu.VMEM((3,) + cut + (D,), bf16),
            pltpu.VMEM((tall, D), f32),
            pltpu.VMEM((3, tall, D), f32),
            pltpu.VMEM((line, 2 * tall, D), bf16),
            pltpu.VMEM((line - 1, 2 * tall, D), bf16),
            pltpu.VMEM((line - 1, 2 * tall, D), bf16),
            pltpu.VMEM((2 * tall, D), f32),
            pltpu.VMEM((2, deep, D), bf16),
            pltpu.VMEM((2, deep, D), bf16),
            pltpu.VMEM((line - 1, 2, deep, D), bf16),
            pltpu.VMEM((2, deep, D), f32),
            pltpu.VMEM(cut + (D,), bf16),
        ]
        + reduce_scratch(line, 2 * tall, D, 1)
        + [pltpu.VMEM((4, 2, deep, D), bf16)]
        + plane_scratch(line, deep, D, 1)
        + reduce_scratch(line, 2 * tall, D // 2, 4)
        + sum_scratch(line, 32)
        + sum_scratch(line, 8)
        + [pltpu.SemaphoreType.DMA((8, 5 + line))] * 2
        + [pltpu.SemaphoreType.DMA((3,)), pltpu.SemaphoreType.DMA((7, 4))],
        compiler_params=pltpu.CompilerParams(
            vmem_limit_bytes=FRONT_LIMIT, collective_id=1, has_side_effects=True
        ),
        name="rear",
    )(tokens, ends, w_both, vec, moments, small, proj, normed, mixed, middle, *terms, *sums, *weights, vectors, bias, *rows)


def plain_device(
    tokens,
    ends,
    cot_out,
    cot_pooled,
    w_qkv,
    w_out,
    w_up,
    w_down,
    vectors,
    bias_up,
    row_qkv,
    col_qkv,
    row_out,
    col_out,
    row_up,
    col_up,
    row_down,
    col_down,
    moment_vectors,
    moment_bias_up,
):
    low_qkv = w_qkv.astype(jnp.bfloat16)
    low_out = w_out.astype(jnp.bfloat16)
    low_up = w_up.astype(jnp.bfloat16)
    low_down = w_down.astype(jnp.bfloat16)
    low_vec = vectors.astype(jnp.bfloat16)
    low_upbias = bias_up.astype(jnp.bfloat16)
    gathered = (
        lax.all_gather(low_qkv, ("dp", "fsdp"), axis=0, tiled=True),
        lax.all_gather(low_out, ("dp", "fsdp"), axis=0, tiled=True),
        lax.all_gather(low_up, ("dp", "fsdp"), axis=0, tiled=True),
        lax.all_gather(low_down, ("dp", "fsdp"), axis=0, tiled=True),
        lax.all_gather(low_vec, ("dp", "fsdp"), axis=0, tiled=True),
        lax.all_gather(low_upbias, ("dp", "fsdp"), axis=0, tiled=True),
    )
    qkv_full, out_full, up_full, down_full = (gathered[0], gathered[1], gathered[2], gathered[3])
    vec_full = gathered[4].astype(jnp.float32)
    upbias_full = gathered[5].astype(jnp.float32)
    vec = vec_full.T
    bias = upbias_full.reshape(1, FF)
    normed, proj, mixed, middle, normed_two = forward_call(tokens, ends, qkv_full, out_full, vec)
    out_tokens, pooled, grad_middle, grad_w_up, grad_w_down, small = feed_call(
        normed_two, middle, up_full, down_full, vec, bias, cot_out, cot_pooled, ends
    )
    grad_tokens, grad_w_qkv, grad_w_out, small = backward_call(
        tokens, ends, qkv_full, out_full, vec, normed, proj, mixed, grad_middle, small
    )
    grad_vectors = small[:8].T
    grad_bias_up = small[8:12].reshape(FF)
    summed_up, summed_down, summed_upbias = (
        lax.psum_scatter(grad_w_up.astype(f32), ("dp", "fsdp"), scatter_dimension=0, tiled=True),
        lax.psum_scatter(grad_w_down.astype(f32), ("dp", "fsdp"), scatter_dimension=0, tiled=True),
        lax.psum_scatter(grad_bias_up, ("dp", "fsdp"), scatter_dimension=0, tiled=True),
    )
    summed_qkv, summed_out, summed_vec = (
        lax.psum_scatter(grad_w_qkv.astype(f32), ("dp", "fsdp"), scatter_dimension=0, tiled=True),
        lax.psum_scatter(grad_w_out.astype(f32), ("dp", "fsdp"), scatter_dimension=0, tiled=True),
        lax.psum_scatter(grad_vectors, ("dp", "fsdp"), scatter_dimension=0, tiled=True),
    )
    matrices = (summed_qkv, summed_out, summed_up, summed_down)
    old_rows = (row_qkv, row_out, row_up, row_down)
    old_cols = (col_qkv, col_out, col_up, col_down)
    masters = (w_qkv, w_out, w_up, w_down)
    row_sizes = (D, D, D, FF)
    tensor_sizes = (3 * D * D, D * D, D * FF, FF * D)
    squares = [gradient * gradient + square_eps for gradient in matrices]
    rows_new = [
        decay * old + (1.0 - decay) * jnp.mean(square, 1) for old, square in zip(old_rows, squares)
    ]
    col_parts = [jnp.sum(square, 0) for square in squares]
    local_totals = jnp.concatenate(
        [
            jnp.stack([jnp.sum(renewed) for renewed in rows_new]),
            jnp.stack([jnp.sum(master * master) for master in masters]),
            jnp.sum(vectors * vectors, 0),
            jnp.sum(bias_up * bias_up)[None],
        ]
    )
    col_sum_qkv, col_sum_out, col_sum_up, col_sum_down, global_totals = lax.psum(
        (col_parts[0], col_parts[1], col_parts[2], col_parts[3], local_totals), ("dp", "fsdp")
    )
    col_sums = (col_sum_qkv, col_sum_out, col_sum_up, col_sum_down)
    cols_new = [
        decay * old + (1.0 - decay) * (summed / count)
        for old, summed, count in zip(old_cols, col_sums, row_sizes)
    ]
    updates = []
    for index_mat in range(4):
        row_mean = global_totals[index_mat] / row_sizes[index_mat]
        renewed_row = rows_new[index_mat]
        renewed_col = cols_new[index_mat]
        updates.append(
            matrices[index_mat] * lax.rsqrt(renewed_row[:, None] * renewed_col[None, :] / row_mean)
        )
    moment_vec = decay * moment_vectors + (1.0 - decay) * (summed_vec * summed_vec + square_eps)
    update_vec = summed_vec * lax.rsqrt(moment_vec)
    moment_upb = decay * moment_bias_up + (1.0 - decay) * (
        summed_upbias * summed_upbias + square_eps
    )
    update_upb = summed_upbias * lax.rsqrt(moment_upb)
    local_norm = jnp.sum(update_vec * update_vec) + jnp.sum(update_upb * update_upb)
    for update in updates:
        local_norm = local_norm + jnp.sum(update * update)
    norm_total = lax.psum(local_norm, ("dp", "fsdp"))
    param_count = 4 * D * D + 2 * D * FF + 8 * D + FF
    clip = jnp.maximum(1.0, jnp.sqrt(norm_total / param_count) / clip_limit)
    new_weights = []
    for index_mat in range(4):
        scale = jnp.maximum(
            scale_floor, jnp.sqrt(global_totals[4 + index_mat] / tensor_sizes[index_mat])
        )
        new_weights.append(masters[index_mat] - step_rate * scale * updates[index_mat] / clip)
    vec_scale = jnp.maximum(scale_floor, jnp.sqrt(global_totals[8:16] / D))[None, :]
    new_vec = vectors - step_rate * vec_scale * update_vec / clip
    upb_scale = jnp.maximum(scale_floor, jnp.sqrt(global_totals[16] / FF))
    new_upb = bias_up - step_rate * upb_scale * update_upb / clip
    return (
        out_tokens,
        pooled,
        grad_tokens,
        summed_qkv,
        rows_new[0],
        cols_new[0],
        new_weights[0],
        summed_out,
        rows_new[1],
        cols_new[1],
        new_weights[1],
        summed_up,
        rows_new[2],
        cols_new[2],
        new_weights[2],
        summed_down,
        rows_new[3],
        cols_new[3],
        new_weights[3],
        summed_vec,
        moment_vec,
        new_vec,
        summed_upbias,
        moment_upb,
        new_upb,
        clip,
    )


def kernels_fit(mesh_shape):
    rows = D // (mesh_shape["dp"] * mesh_shape["fsdp"])
    return mesh_shape["fsdp"] == 4 and mesh_shape["dp"] == 8 and rows % 8 == 0


def per_device(
    mesh_shape,
    tokens,
    ends,
    cot_out,
    cot_pooled,
    w_qkv,
    w_out,
    w_up,
    w_down,
    vectors,
    bias_up,
    row_qkv,
    col_qkv,
    row_out,
    col_out,
    row_up,
    col_up,
    row_down,
    col_down,
    moment_vectors,
    moment_bias_up,
):
    def whole(array):
        return array.reshape(-1, array.shape[-1])

    def row(array):
        return array.reshape(1, -1)

    bias_row = row(bias_up)
    moments = (moment_vectors.T, row(moment_bias_up))
    both, normed, proj, mixed, out_tokens, grad_middle, *terms, vec, all_moments, pooled, small, a, b, e, f = front_call(
        mesh_shape, tokens, ends, cot_out, cot_pooled, w_qkv, w_out, w_up, w_down, vectors.T, bias_row, *moments
    )
    weights = (w_qkv, w_out, w_up, w_down)
    rows = [row(value) for value in (row_qkv, row_out, row_up, row_down)]
    cols = [col_qkv, col_out, col_up, col_down]
    grad_tokens, *summed = rear_call(
        mesh_shape, tokens, ends, both, vec, all_moments, small, proj, normed, mixed, grad_middle,
        terms, (a, b, e, f), weights, vectors.T, bias_row, rows
    )
    large = (out_tokens, pooled, grad_tokens)
    done = finish_call(large, summed, weights, vectors.T, bias_row, rows, cols, *moments)
    results, done = list(done[:3]), done[3:]
    for index in range(4):
        results += [done[index], done[4 + index].reshape(-1), done[8 + index], done[12 + index]]
    results += [value.T for value in done[16:19]] + [value.reshape(-1) for value in done[19:22]]
    return tuple(results + [done[22].reshape(())])


def solution(mesh):
    in_specs = (
        P(("dp", "fsdp"), None),
        P(("dp", "fsdp"), None),
        P(("dp", "fsdp"), None),
        P(("dp", "fsdp"), None, None),
        P(("dp", "fsdp"), None),
        P(("dp", "fsdp"), None),
        P(("dp", "fsdp"), None),
        P(("dp", "fsdp"), None),
        P(("dp", "fsdp"), None),
        P(("dp", "fsdp")),
        P(("dp", "fsdp")),
        P(),
        P(("dp", "fsdp")),
        P(),
        P(("dp", "fsdp")),
        P(),
        P(("dp", "fsdp")),
        P(),
        P(("dp", "fsdp"), None),
        P(("dp", "fsdp")),
    )
    out_specs = (
        P(("dp", "fsdp"), None),
        P(("dp", "fsdp"), None, None),
        P(("dp", "fsdp"), None),
        P(("dp", "fsdp"), None),
        P(("dp", "fsdp")),
        P(),
        P(("dp", "fsdp"), None),
        P(("dp", "fsdp"), None),
        P(("dp", "fsdp")),
        P(),
        P(("dp", "fsdp"), None),
        P(("dp", "fsdp"), None),
        P(("dp", "fsdp")),
        P(),
        P(("dp", "fsdp"), None),
        P(("dp", "fsdp"), None),
        P(("dp", "fsdp")),
        P(),
        P(("dp", "fsdp"), None),
        P(("dp", "fsdp"), None),
        P(("dp", "fsdp"), None),
        P(("dp", "fsdp"), None),
        P(("dp", "fsdp")),
        P(("dp", "fsdp")),
        P(("dp", "fsdp")),
        P(),
    )
    fits = kernels_fit(mesh.shape)
    step = functools.partial(per_device, dict(mesh.shape)) if fits else plain_device
    return jax.shard_map(
        step, mesh=mesh, in_specs=in_specs, out_specs=out_specs, check_vma=False
    )
```
